32 devices in a mesh: grp: 2 (over x), row: 16 (over z, y, core).
Axes of the slice: x: 2, y: 2, z: 4, core: 2. Of those that a mesh axis runs over, the one named last changes fastest.
Arguments:
- tile_blocks: bfloat16 [576, 128, 128], P(('grp', 'row')), parts along dimension 0, may hold values from 0 to 1
- q_block: bfloat16 [8192, 128], P(('grp', 'row')), parts along dimension 0, may hold values from -6 to 6
- tile_index: int32 [576, 2], P(('grp', 'row')), parts along dimension 0, may hold values from 0 to 31, as said below
- tile_count: int32 [64], P(('grp', 'row')), parts along dimension 0, may hold values from 1 to 9, as said below
Outputs:
- product: float32 [8192, 128], P(('grp', 'row')), parts along dimension 0
The draws below stay inside these ranges and needn't reach their ends.
There are 2 independent parts, one for each index of `grp`. The reference program is written for one: setup_inputs(seed, part) draws one part's arguments, and reference() takes and returns one part's arrays. A program takes and returns all parts, laid end to end along the dimension named above; each array names one. Nothing has to cross between parts.
Inputs may be any that keep to these rules, and one draw needn't show every extreme that they name: `tile_index`: block rows of a device are 2 d and 2 d + 1; its live slots come first, those of its first block row before those of its second; every live slot has i equal to one of the device's block rows and j >= i, and the live (i, j) of a block row are distinct and include (i, i). Dead slots hold indices of the same form. Device 0 has all 18 slots live. `tile_count`: the sum over a device's 2 block rows is at most 18; block row i has at most 32 - i tiles.
All inputs are finite; a program needn't handle non-finite values.
Results may differ from the reference program's by a relative error of at most 0.0003.
Values may be sent and summed in bfloat16 or wider, within the bound.
No kernel may reach another device: no remote copies, remote signals or barrier semaphores. Data moves between devices by JAX's collectives and lax.ppermute only.
A program may use at most 128 MiB of HBM per device.

```python
import jax
import jax.numpy as jnp
from jax import lax

TILE = 128
K = 128
BLK = 2
NBLK = 32
NODES = 4096
SLOTS = 18


def layout(key):
    first_key, second_key = jax.random.split(key)
    row_ids = jnp.arange(NBLK, dtype=jnp.int32)
    fraction = jax.random.randint(first_key, (NBLK,), 1, 3, dtype=jnp.int32)
    counts = jnp.maximum(1, (NBLK - row_ids) * fraction // 10).astype(jnp.int32)
    counts = counts.at[0].set(SLOTS // 2).at[1].set(SLOTS - SLOTS // 2)
    scores = jax.random.randint(second_key, (NBLK, NBLK), 0, 2 ** 20, dtype=jnp.int32)
    column_ids = jnp.arange(NBLK, dtype=jnp.int32)[None, :]
    scores = scores * NBLK + column_ids
    scores = jnp.where(column_ids == row_ids[:, None], -1, scores)
    scores = jnp.where(column_ids < row_ids[:, None], 2 ** 30, scores)
    ranking = jnp.argsort(scores, axis=1).astype(jnp.int32)
    device_total = NBLK // BLK
    first_rows = BLK * jnp.arange(device_total, dtype=jnp.int32)[:, None]
    second_rows = first_rows + 1
    slot_ids = jnp.arange(SLOTS, dtype=jnp.int32)[None, :]
    first_count = counts[first_rows]
    in_first = slot_ids < first_count
    first_cols = jnp.take_along_axis(ranking[first_rows[:, 0]], jnp.clip(slot_ids, 0, NBLK - 1) * jnp.ones_like(first_rows), axis=1)
    spare = NBLK - second_rows
    later = jnp.maximum(slot_ids - first_count, 0) % spare
    second_cols = jnp.take_along_axis(ranking[second_rows[:, 0]], later, axis=1)
    rows = jnp.where(in_first, first_rows, second_rows)
    cols = jnp.where(in_first, first_cols, second_cols)
    table = jnp.stack([rows, cols], axis=-1).reshape(device_total * SLOTS, 2).astype(jnp.int32)
    return (table, counts)


def draw_tile_index(key, part):
    table, counts = layout(key)
    return table


def draw_tile_count(key, part):
    table, counts = layout(key)
    return counts


def levels(stream_key, shape, cuts, least, top_value):
    def one(dim, parts):
        heights = jax.random.uniform(jax.random.fold_in(jax.random.fold_in(stream_key, 6), dim), (parts,), jnp.float32, least / len(cuts), top_value / len(cuts))
        return jnp.repeat(jnp.exp(heights), shape[dim] // parts).reshape((-1,) + (1,) * (len(shape) - dim - 1))

    factor_of = one(*cuts[0])
    for cut in cuts[1:]:
        factor_of = factor_of * one(*cut)
    return factor_of


def bell_draw(stream_key, shape, scale, bound, cuts=(), held_as=jnp.bfloat16):
    result = scale * jax.random.normal(stream_key, shape, jnp.float32)
    if cuts:
        result = result * levels(stream_key, shape, cuts, -0.22, 0.18)
    return jnp.clip(result, -bound, bound).astype(held_as)


def setup_inputs(seed: int = 0, part: int = 0) -> dict:
    keys = jax.random.split(jax.random.key(seed), 5)
    part_splits = jax.random.split(jax.random.fold_in(keys[4], part), 5)
    return {
        "tile_blocks": jnp.clip(1.0 * jax.random.uniform(part_splits[0], (NBLK * SLOTS // BLK, TILE, TILE), jnp.float32) ** levels(part_splits[0], (NBLK * SLOTS // BLK, TILE, TILE), ((0, 16),), -0.2, 0.2), 0.0, 1.0).astype(jnp.bfloat16),
        "q_block": bell_draw(part_splits[1], (NODES, K), 1.0, 6.0, ((0, 16),)),
        "tile_index": draw_tile_index(jax.random.fold_in(jax.random.fold_in(keys[4], part), 71), part),
        "tile_count": draw_tile_count(jax.random.fold_in(jax.random.fold_in(keys[4], part), 71), part),
    }


def reference(tile_blocks, q_block, tile_index, tile_count):
    device_total = NBLK // BLK
    basis = q_block.astype(jnp.float32).reshape(NBLK, TILE, K)
    stacked = tile_blocks.reshape(device_total, SLOTS, TILE, TILE)
    indices = tile_index.reshape(device_total, SLOTS, 2)
    live_totals = lax.optimization_barrier(jnp.sum(tile_count.reshape(device_total, BLK), axis=1))

    def add_device(accum, slot_item):
        blocks, index_pair, live_total = slot_item
        row_block = index_pair[:, 0]
        col_block = index_pair[:, 1]
        weights = (jnp.arange(SLOTS) < live_total).astype(jnp.float32)[:, None, None]
        matrices = blocks.astype(jnp.float32)
        direct = jnp.einsum('sab,sbk->sak', matrices, basis[col_block], precision=lax.Precision.HIGHEST) * weights
        mirrored = jnp.einsum('sab,sak->sbk', matrices, basis[row_block], precision=lax.Precision.HIGHEST) * weights
        accum = accum + jax.ops.segment_sum(direct, row_block, num_segments=NBLK)
        accum = accum + jax.ops.segment_sum(mirrored, col_block, num_segments=NBLK)
        return (accum, None)
    total, _ = lax.scan(add_device, jnp.zeros((NBLK, TILE, K), jnp.float32), (stacked, indices, live_totals))
    return total.reshape(NBLK * TILE, K) / jnp.sqrt(jnp.float32(NBLK * TILE))
```

```python
import functools
import math

import jax
import jax.numpy as jnp
from jax import lax
from jax.experimental import pallas as pl
from jax.experimental.pallas import tpu as pltpu
from jax.sharding import PartitionSpec as P

TOP = 32700.0
STEPS = 16.0
LEAST = 1e-30


def place():
    me = lax.axis_index("row")
    return me // 2, me % 2


def scale_of(code):
    return jnp.exp2(code * (1.0 / STEPS))


def encode(x):
    top = jnp.maximum(jnp.max(jnp.abs(x), axis=0, keepdims=True), LEAST)
    code = jnp.ceil(jnp.log2(top) * STEPS)
    values = jnp.round(x * (TOP / scale_of(code)))
    return values.astype(jnp.int32).astype(jnp.int16), code


def pack_kernel(
    own_index, own_count, other_index, other_count, own_tiles, other_tiles,
    own_q, other_q, *outs,
):
    *messages, panels, chip_q, local_rows = outs
    slots = len(messages)
    tile = own_tiles.shape[1]
    rows = own_q.shape[0]
    chip_blocks = 2 * rows // tile
    chip, core = place()

    panels[...] = jnp.zeros_like(panels)
    for index, count, tiles in (
        (own_index, own_count, own_tiles),
        (other_index, other_count, other_tiles),
    ):
        live = count[0]
        for r in range(1, count.shape[0]):
            live = live + count[r]

        def put(s, carry, index=index, tiles=tiles):
            i, j = index[s, 0], index[s, 1]
            cls = chip ^ (j // chip_blocks)

            @pl.when(cls % 2 == core)
            def _():
                panel = (cls // 2) * chip_blocks + j % chip_blocks
                at = pl.multiple_of((i % chip_blocks) * tile, tile)
                panels[panel, pl.ds(at, tile), :] = tiles[s]

            return carry

        lax.fori_loop(0, live, put, 0)

    chip_q[pl.ds(pl.multiple_of(core * rows, rows), rows), :] = own_q[...]
    chip_q[pl.ds(pl.multiple_of((1 - core) * rows, rows), rows), :] = other_q[...]
    q = chip_q[...]
    q_t = q.T
    q_wide = q.astype(jnp.float32)
    for k in reversed(range(slots)):
        up = chip < (chip ^ (2 * k + core))
        codes = []
        for b in range(0, chip_blocks, 2):
            g = k * chip_blocks + b
            pair = jnp.concatenate([panels[g], panels[g + 1]], axis=1)
            sums = jnp.dot(q_t, pair, preferred_element_type=jnp.float32)
            for e in range(2):
                block = sums[:, e * tile:(e + 1) * tile]
                at = (b + e) * tile
                if k == 0:
                    local_rows[at:at + tile, :] = block
                x = jnp.where(up, block, q_wide[at:at + tile, :])
                values, code = encode(x)
                messages[k][at:at + tile, :] = values
                codes.append(code)
        which = lax.broadcasted_iota(jnp.int32, (16, tile), 0)
        tail = jnp.zeros((16, tile), jnp.float32)
        for b, code in enumerate(codes):
            tail = jnp.where(which == b, code, tail)
        messages[k][chip_blocks * tile:, :] = tail.astype(jnp.int32).astype(jnp.int16)


def local_kernel(panels, chip_q, local_rows, base):
    chip_blocks, rows, tile = panels.shape
    _, core = place()
    mine = core == 0
    total = jnp.zeros((rows, tile), jnp.float32)
    for b in range(0, chip_blocks, 2):
        pair = jnp.concatenate([panels[b], panels[b + 1]], axis=1)
        total += jnp.dot(
            pair, chip_q[b * tile:(b + 2) * tile, :], preferred_element_type=jnp.float32
        )
    for b in range(chip_blocks):
        at = slice(b * tile, (b + 1) * tile)
        base[at, :] = jnp.where(mine, total[at, :] + local_rows[at, :].T, 0.0)


def unpack_kernel(base, panels, *refs):
    *received, keep, send, result = refs
    tile = panels.shape[2]
    chip_rows = panels.shape[1]
    chip_blocks = chip_rows // tile
    rows = chip_rows // 2
    chip, core = place()
    total = base[...]
    mirrored = [jnp.zeros((tile, tile), jnp.float32) for _ in range(chip_blocks)]
    for k in reversed(range(len(received))):
        message = received[k]
        low = (chip ^ (2 * k + core)) < chip
        tail = message[chip_rows:, :].astype(jnp.int32).astype(jnp.float32)
        scales = scale_of(tail) * (1.0 / TOP)
        for b in range(0, chip_blocks, 2):
            parts = []
            for e in (b, b + 1):
                values = message[e * tile:(e + 1) * tile, :]
                x = values.astype(jnp.int32).astype(jnp.float32) * scales[e:e + 1, :]
                mirrored[e] += jnp.where(low, x, 0.0)
                parts.append(x.astype(jnp.bfloat16))
            g = k * chip_blocks + b
            pair = jnp.concatenate([panels[g], panels[g + 1]], axis=1)
            total += jnp.dot(
                pair, jnp.concatenate(parts, axis=0), preferred_element_type=jnp.float32
            )
    for b in range(chip_blocks):
        at = slice(b * tile, (b + 1) * tile)
        result[at, :] = total[at, :] + mirrored[b].T
    keep[...] = result[pl.ds(pl.multiple_of(core * rows, rows), rows), :]
    send[...] = result[pl.ds(pl.multiple_of((1 - core) * rows, rows), rows), :]


VMEM = functools.partial(pl.BlockSpec, memory_space=pltpu.VMEM)
SMEM = functools.partial(pl.BlockSpec, memory_space=pltpu.SMEM)


def on_device(devices, tile_blocks, q_block, tile_index, tile_count):
    tile = tile_blocks.shape[1]
    rows, columns = q_block.shape
    chips = devices // 2
    slots = chips // 2
    chip_rows = 2 * rows
    chip_blocks = chip_rows // tile
    wide = jnp.float32
    other_core = [(d, d ^ 1) for d in range(devices)]

    def swap(x):
        return lax.ppermute(x, "row", other_core)

    other_tiles = swap(tile_blocks)
    other_q = swap(q_block)
    other_index = swap(tile_index)
    other_count = swap(tile_count)

    message = jax.ShapeDtypeStruct((chip_rows + 16, columns), jnp.int16)
    *messages, panels, chip_q, local_rows = pl.pallas_call(
        pack_kernel,
        out_shape=[message] * slots + [
            jax.ShapeDtypeStruct((slots * chip_blocks, chip_rows, tile), jnp.bfloat16),
            jax.ShapeDtypeStruct((chip_rows, columns), jnp.bfloat16),
            jax.ShapeDtypeStruct((chip_rows, columns), wide),
        ],
        in_specs=[SMEM()] * 4 + [VMEM()] * 4,
        out_specs=[VMEM()] * (slots + 3),
        compiler_params=pltpu.CompilerParams(vmem_limit_bytes=48 * 2**20),
        name="pack",
    )(tile_index, tile_count, other_index, other_count, tile_blocks, other_tiles,
      q_block, other_q)

    received = [None] * slots
    for k in reversed(range(slots)):
        pairs = [
            (d, d ^ (2 * (2 * k + d % 2))) for d in range(devices) if 2 * k + d % 2
        ]
        received[k] = lax.ppermute(messages[k], "row", pairs)

    base = pl.pallas_call(
        local_kernel,
        out_shape=jax.ShapeDtypeStruct((chip_rows, columns), wide),
        in_specs=[VMEM()] * 3,
        out_specs=VMEM(),
        compiler_params=pltpu.CompilerParams(vmem_limit_bytes=32 * 2**20),
        name="local",
    )(panels[:chip_blocks], chip_q, local_rows)

    keep, send = pl.pallas_call(
        unpack_kernel,
        out_shape=[jax.ShapeDtypeStruct((rows, columns), wide)] * 2,
        in_specs=[VMEM()] * (2 + slots),
        out_specs=[VMEM()] * 2,
        scratch_shapes=[pltpu.VMEM((chip_rows, columns), wide)],
        compiler_params=pltpu.CompilerParams(vmem_limit_bytes=48 * 2**20),
        name="unpack",
    )(base, panels, *received)
    return (keep + swap(send)) * (1.0 / math.sqrt(rows * devices))


def solution(mesh):
    return jax.shard_map(
        functools.partial(on_device, mesh.shape["row"]),
        mesh=mesh,
        in_specs=(
            P(("grp", "row"), None, None),
            P(("grp", "row"), None),
            P(("grp", "row"), None),
            P(("grp", "row")),
        ),
        out_specs=P(("grp", "row"), None),
        check_vma=False,
    )
```

```python
import functools
import math

import jax
import jax.numpy as jnp
from jax import lax
from jax.experimental import pallas as pl
from jax.experimental.pallas import tpu as pltpu
from jax.sharding import PartitionSpec as P

TOP = 32700.0
STEPS = 16.0
LEAST = 1e-30


def place():
    me = lax.axis_index("row")
    return me // 2, me % 2


def scale_of(code):
    return jnp.exp2(code * (1.0 / STEPS))


def encode(x):
    top = jnp.maximum(jnp.max(jnp.abs(x), axis=0, keepdims=True), LEAST)
    code = jnp.ceil(jnp.log2(top) * STEPS)
    values = jnp.round(x * (TOP / scale_of(code)))
    return values.astype(jnp.int32).astype(jnp.int16), code


def put_tiles(index, count, tiles, panels, chip_blocks):
    chip, core = place()
    tile = tiles.shape[1]
    live = count[0]
    for r in range(1, count.shape[0]):
        live = live + count[r]

    def put(s, carry):
        i, j = index[0, s], index[1, s]
        cls = chip ^ (j // chip_blocks)

        @pl.when(cls % 2 == core)
        def _():
            panel = (cls // 2) * chip_blocks + j % chip_blocks
            at = pl.multiple_of((i % chip_blocks) * tile, tile)
            panels[panel, pl.ds(at, tile), :] = tiles[s]

        return carry

    lax.fori_loop(0, live, put, 0)


def own_kernel(index, count, tiles, panels):
    panels[...] = jnp.zeros_like(panels)
    put_tiles(index, count, tiles, panels, panels.shape[1] // panels.shape[2])


def write_messages(slots, panels, chip_q, messages, local_rows=None):
    chip_rows, tile = panels.shape[1:]
    chip_blocks = chip_rows // tile
    chip, core = place()
    q = chip_q[...]
    q_t = q.T
    q_wide = q.astype(jnp.float32)
    for k, message in zip(slots, messages, strict=True):
        up = chip < (chip ^ (2 * k + core))
        codes = []
        for b in range(0, chip_blocks, 2):
            g = k * chip_blocks + b
            pair = jnp.concatenate([panels[g], panels[g + 1]], axis=1)
            sums = jnp.dot(q_t, pair, preferred_element_type=jnp.float32)
            for e in range(2):
                block = sums[:, e * tile:(e + 1) * tile]
                at = (b + e) * tile
                if k == 0:
                    local_rows[at:at + tile, :] = block
                x = jnp.where(up, block, q_wide[at:at + tile, :])
                values, code = encode(x)
                message[at:at + tile, :] = values
                codes.append(code)
        which = lax.broadcasted_iota(jnp.int32, (16, tile), 0)
        tail = jnp.zeros((16, tile), jnp.float32)
        for b, code in enumerate(codes):
            tail = jnp.where(which == b, code, tail)
        message[chip_rows:, :] = tail.astype(jnp.int32).astype(jnp.int16)


def far_kernel(slots, index, count, tiles, own_q, other_q, _, panels, chip_q, *messages):
    rows = own_q.shape[0]
    _, core = place()
    put_tiles(index, count, tiles, panels, panels.shape[1] // panels.shape[2])
    chip_q[pl.ds(pl.multiple_of(core * rows, rows), rows), :] = own_q[...]
    chip_q[pl.ds(pl.multiple_of((1 - core) * rows, rows), rows), :] = other_q[...]
    write_messages(slots, panels, chip_q, messages)


def near_kernel(slots, panels, chip_q, local_rows, *messages):
    write_messages(slots, panels, chip_q, messages, local_rows)


def local_kernel(panels, chip_q, local_rows, base):
    chip_blocks, rows, tile = panels.shape
    _, core = place()
    mine = core == 0
    total = jnp.zeros((rows, tile), jnp.float32)
    for b in range(0, chip_blocks, 2):
        pair = jnp.concatenate([panels[b], panels[b + 1]], axis=1)
        total += jnp.dot(
            pair, chip_q[b * tile:(b + 2) * tile, :], preferred_element_type=jnp.float32
        )
    for b in range(chip_blocks):
        at = slice(b * tile, (b + 1) * tile)
        base[at, :] = jnp.where(mine, total[at, :] + local_rows[at, :].T, 0.0)


def unpack_kernel(base, panels, *refs):
    *received, keep, send, result = refs
    tile = panels.shape[2]
    chip_rows = panels.shape[1]
    chip_blocks = chip_rows // tile
    rows = chip_rows // 2
    chip, core = place()
    total = base[...]
    mirrored = [jnp.zeros((tile, tile), jnp.float32) for _ in range(chip_blocks)]
    for k in reversed(range(len(received))):
        message = received[k]
        low = (chip ^ (2 * k + core)) < chip
        tail = message[chip_rows:, :].astype(jnp.int32).astype(jnp.float32)
        scales = scale_of(tail) * (1.0 / TOP)
        for b in range(0, chip_blocks, 2):
            parts = []
            for e in (b, b + 1):
                values = message[e * tile:(e + 1) * tile, :]
                x = values.astype(jnp.int32).astype(jnp.float32) * scales[e:e + 1, :]
                mirrored[e] += jnp.where(low, x, 0.0)
                parts.append(x.astype(jnp.bfloat16))
            g = k * chip_blocks + b
            pair = jnp.concatenate([panels[g], panels[g + 1]], axis=1)
            total += jnp.dot(
                pair, jnp.concatenate(parts, axis=0), preferred_element_type=jnp.float32
            )
    for b in range(chip_blocks):
        at = slice(b * tile, (b + 1) * tile)
        result[at, :] = total[at, :] + mirrored[b].T
    keep[...] = result[pl.ds(pl.multiple_of(core * rows, rows), rows), :]
    send[...] = result[pl.ds(pl.multiple_of((1 - core) * rows, rows), rows), :]


VMEM = functools.partial(pl.BlockSpec, memory_space=pltpu.VMEM)
SMEM = functools.partial(pl.BlockSpec, memory_space=pltpu.SMEM)


def on_device(devices, tile_blocks, q_block, tile_index, tile_count):
    tile = tile_blocks.shape[1]
    rows, columns = q_block.shape
    chips = devices // 2
    slots = chips // 2
    chip_rows = 2 * rows
    chip_blocks = chip_rows // tile
    wide = jnp.float32
    other_core = [(d, d ^ 1) for d in range(devices)]

    def swap(x):
        return lax.ppermute(x, "row", other_core)

    index = tile_index.T
    other_tiles = swap(tile_blocks)
    other_q = swap(q_block)
    other_index = swap(index)
    other_count = swap(tile_count)

    panels_shape = jax.ShapeDtypeStruct(
        (slots * chip_blocks, chip_rows, tile), jnp.bfloat16
    )
    q_shape = jax.ShapeDtypeStruct((chip_rows, columns), jnp.bfloat16)
    message = jax.ShapeDtypeStruct((chip_rows + 16, columns), jnp.int16)
    params = pltpu.CompilerParams(vmem_limit_bytes=48 * 2**20)
    own_panels = pl.pallas_call(
        own_kernel,
        out_shape=panels_shape,
        in_specs=[SMEM(), SMEM(), pl.BlockSpec()],
        out_specs=VMEM(),
        compiler_params=params,
        name="own_tiles",
    )(index, tile_count, tile_blocks)
    near = list(reversed(range(slots // 2)))
    far = list(reversed(range(slots // 2, slots)))
    panels, chip_q, *far_messages = pl.pallas_call(
        functools.partial(far_kernel, far),
        out_shape=[panels_shape, q_shape] + [message] * len(far),
        in_specs=[SMEM(), SMEM(), VMEM(), pl.BlockSpec(), VMEM(), VMEM()],
        out_specs=[VMEM()] * (2 + len(far)),
        input_output_aliases={5: 0},
        compiler_params=params,
        name="pack_far",
    )(other_index, other_count, other_tiles, q_block, other_q, own_panels)
    local_rows, *near_messages = pl.pallas_call(
        functools.partial(near_kernel, near),
        out_shape=[jax.ShapeDtypeStruct((chip_rows, columns), wide)] + [message] * len(near),
        in_specs=[VMEM()] * 2,
        out_specs=[VMEM()] * (1 + len(near)),
        compiler_params=params,
        name="pack_near",
    )(panels, chip_q)
    messages = dict(zip(far + near, far_messages + near_messages, strict=True))

    received = [None] * slots
    for k in reversed(range(slots)):
        pairs = [
            (d, d ^ (2 * (2 * k + d % 2))) for d in range(devices) if 2 * k + d % 2
        ]
        received[k] = lax.ppermute(messages[k], "row", pairs)

    base = pl.pallas_call(
        local_kernel,
        out_shape=jax.ShapeDtypeStruct((chip_rows, columns), wide),
        in_specs=[VMEM()] * 3,
        out_specs=VMEM(),
        compiler_params=pltpu.CompilerParams(vmem_limit_bytes=32 * 2**20),
        name="local",
    )(panels[:chip_blocks], chip_q, local_rows)

    keep, send = pl.pallas_call(
        unpack_kernel,
        out_shape=[jax.ShapeDtypeStruct((rows, columns), wide)] * 2,
        in_specs=[VMEM()] * (2 + slots),
        out_specs=[VMEM()] * 2,
        scratch_shapes=[pltpu.VMEM((chip_rows, columns), wide)],
        compiler_params=pltpu.CompilerParams(vmem_limit_bytes=48 * 2**20),
        name="unpack",
    )(base, panels, *received)
    return (keep + swap(send)) * (1.0 / math.sqrt(rows * devices))


def solution(mesh):
    return jax.shard_map(
        functools.partial(on_device, mesh.shape["row"]),
        mesh=mesh,
        in_specs=(
            P(("grp", "row"), None, None),
            P(("grp", "row"), None),
            P(("grp", "row"), None),
            P(("grp", "row")),
        ),
        out_specs=P(("grp", "row"), None),
        check_vma=False,
    )
```

```python
import functools
import math

import jax
import jax.numpy as jnp
from jax import lax
from jax.experimental import pallas as pl
from jax.experimental.pallas import tpu as pltpu
from jax.sharding import PartitionSpec as P

TOP = 32700.0
STEPS = 16.0
LEAST = 1e-30


def place():
    me = lax.axis_index("row")
    return me // 2, me % 2


def scale_of(code):
    return jnp.exp2(code * (1.0 / STEPS))


def encode(x):
    top = jnp.maximum(jnp.max(jnp.abs(x), axis=0, keepdims=True), LEAST)
    code = jnp.ceil(jnp.log2(top) * STEPS)
    values = jnp.round(x * (TOP / scale_of(code)))
    return values.astype(jnp.int32).astype(jnp.int16), code


def put_tiles(index, count, tiles, panels, chip_blocks):
    chip, core = place()
    tile = tiles.shape[1]
    live = count[0]
    for r in range(1, count.shape[0]):
        live = live + count[r]

    def put(s, carry):
        i, j = index[0, s], index[1, s]
        cls = chip ^ (j // chip_blocks)

        @pl.when(cls % 2 == core)
        def _():
            panel = (cls // 2) * chip_blocks + j % chip_blocks
            at = pl.multiple_of((i % chip_blocks) * tile, tile)
            panels[panel, pl.ds(at, tile), :] = tiles[s]

        return carry

    lax.fori_loop(0, live, put, 0)


def own_kernel(index_ref, count_ref, tiles_ref, panels, index, count, tiles, sems):
    copies = [
        pltpu.make_async_copy(a, b, sems.at[n])
        for n, (a, b) in enumerate(
            ((index_ref, index), (count_ref, count), (tiles_ref, tiles))
        )
    ]
    for copy in copies:
        copy.start()
    panels[...] = jnp.zeros_like(panels)
    for copy in copies:
        copy.wait()
    put_tiles(index, count, tiles, panels, panels.shape[1] // panels.shape[2])


def write_messages(slots, panels, chip_q, messages, local_rows=None):
    chip_rows, tile = panels.shape[1:]
    chip_blocks = chip_rows // tile
    chip, core = place()
    q = chip_q[...]
    q_t = q.T
    q_wide = q.astype(jnp.float32)
    for k, message in zip(slots, messages, strict=True):
        up = chip < (chip ^ (2 * k + core))
        codes = []
        for b in range(0, chip_blocks, 2):
            g = k * chip_blocks + b
            pair = jnp.concatenate([panels[g], panels[g + 1]], axis=1)
            sums = jnp.dot(q_t, pair, preferred_element_type=jnp.float32)
            for e in range(2):
                block = sums[:, e * tile:(e + 1) * tile]
                at = (b + e) * tile
                if k == 0:
                    local_rows[at:at + tile, :] = block
                x = jnp.where(up, block, q_wide[at:at + tile, :])
                values, code = encode(x)
                message[at:at + tile, :] = values
                codes.append(code)
        which = lax.broadcasted_iota(jnp.int32, (16, tile), 0)
        tail = jnp.zeros((16, tile), jnp.float32)
        for b, code in enumerate(codes):
            tail = jnp.where(which == b, code, tail)
        message[chip_rows:, :] = tail.astype(jnp.int32).astype(jnp.int16)


def far_kernel(slots, index, count, tiles, own_q, other_q, _, panels, chip_q, *messages):
    rows = own_q.shape[0]
    _, core = place()
    put_tiles(index, count, tiles, panels, panels.shape[1] // panels.shape[2])
    chip_q[pl.ds(pl.multiple_of(core * rows, rows), rows), :] = own_q[...]
    chip_q[pl.ds(pl.multiple_of((1 - core) * rows, rows), rows), :] = other_q[...]
    write_messages(slots, panels, chip_q, messages)


def near_kernel(slots, panels, chip_q, local_rows, *messages):
    write_messages(slots, panels, chip_q, messages, local_rows)


def local_kernel(panels, chip_q, local_rows, base):
    chip_blocks, rows, tile = panels.shape
    _, core = place()
    mine = core == 0
    total = jnp.zeros((rows, tile), jnp.float32)
    for b in range(0, chip_blocks, 2):
        pair = jnp.concatenate([panels[b], panels[b + 1]], axis=1)
        total += jnp.dot(
            pair, chip_q[b * tile:(b + 2) * tile, :], preferred_element_type=jnp.float32
        )
    for b in range(chip_blocks):
        at = slice(b * tile, (b + 1) * tile)
        base[at, :] = jnp.where(mine, total[at, :] + local_rows[at, :].T, 0.0)


def unpack_kernel(base, panels, *refs):
    *received, keep, send, result = refs
    tile = panels.shape[2]
    chip_rows = panels.shape[1]
    chip_blocks = chip_rows // tile
    rows = chip_rows // 2
    chip, core = place()
    total = base[...]
    mirrored = [jnp.zeros((tile, tile), jnp.float32) for _ in range(chip_blocks)]
    for k in reversed(range(len(received))):
        message = received[k]
        low = (chip ^ (2 * k + core)) < chip
        tail = message[chip_rows:, :].astype(jnp.int32).astype(jnp.float32)
        scales = scale_of(tail) * (1.0 / TOP)
        for b in range(0, chip_blocks, 2):
            parts = []
            for e in (b, b + 1):
                values = message[e * tile:(e + 1) * tile, :]
                x = values.astype(jnp.int32).astype(jnp.float32) * scales[e:e + 1, :]
                mirrored[e] += jnp.where(low, x, 0.0)
                parts.append(x.astype(jnp.bfloat16))
            g = k * chip_blocks + b
            pair = jnp.concatenate([panels[g], panels[g + 1]], axis=1)
            total += jnp.dot(
                pair, jnp.concatenate(parts, axis=0), preferred_element_type=jnp.float32
            )
    for b in range(chip_blocks):
        at = slice(b * tile, (b + 1) * tile)
        result[at, :] = total[at, :] + mirrored[b].T
    keep[...] = result[pl.ds(pl.multiple_of(core * rows, rows), rows), :]
    send[...] = result[pl.ds(pl.multiple_of((1 - core) * rows, rows), rows), :]


VMEM = functools.partial(pl.BlockSpec, memory_space=pltpu.VMEM)
SMEM = functools.partial(pl.BlockSpec, memory_space=pltpu.SMEM)


def on_device(devices, tile_blocks, q_block, tile_index, tile_count):
    tile = tile_blocks.shape[1]
    rows, columns = q_block.shape
    chips = devices // 2
    slots = chips // 2
    chip_rows = 2 * rows
    chip_blocks = chip_rows // tile
    wide = jnp.float32
    other_core = [(d, d ^ 1) for d in range(devices)]

    def swap(x):
        return lax.ppermute(x, "row", other_core)

    index = tile_index.T
    other_tiles = swap(tile_blocks)
    other_q = swap(q_block)
    other_index = swap(index)
    other_count = swap(tile_count)

    panels_shape = jax.ShapeDtypeStruct(
        (slots * chip_blocks, chip_rows, tile), jnp.bfloat16
    )
    q_shape = jax.ShapeDtypeStruct((chip_rows, columns), jnp.bfloat16)
    message = jax.ShapeDtypeStruct((chip_rows + 16, columns), jnp.int16)
    params = pltpu.CompilerParams(vmem_limit_bytes=48 * 2**20)
    own_panels = pl.pallas_call(
        own_kernel,
        out_shape=panels_shape,
        in_specs=[pl.BlockSpec(memory_space=pltpu.HBM)] * 3,
        out_specs=VMEM(),
        scratch_shapes=[
            pltpu.SMEM(index.shape, index.dtype),
            pltpu.SMEM(tile_count.shape, tile_count.dtype),
            pltpu.VMEM(tile_blocks.shape, tile_blocks.dtype),
            pltpu.SemaphoreType.DMA((3,)),
        ],
        compiler_params=params,
        name="own_tiles",
    )(*(pltpu.with_memory_space_constraint(a, pltpu.HBM) for a in (index, tile_count, tile_blocks)))
    near = list(reversed(range(slots // 2)))
    far = list(reversed(range(slots // 2, slots)))
    panels, chip_q, *far_messages = pl.pallas_call(
        functools.partial(far_kernel, far),
        out_shape=[panels_shape, q_shape] + [message] * len(far),
        in_specs=[SMEM(), SMEM(), VMEM(), pl.BlockSpec(), VMEM(), VMEM()],
        out_specs=[VMEM()] * (2 + len(far)),
        input_output_aliases={5: 0},
        compiler_params=params,
        name="pack_far",
    )(other_index, other_count, other_tiles, q_block, other_q, own_panels)
    local_rows, *near_messages = pl.pallas_call(
        functools.partial(near_kernel, near),
        out_shape=[jax.ShapeDtypeStruct((chip_rows, columns), wide)] + [message] * len(near),
        in_specs=[VMEM()] * 2,
        out_specs=[VMEM()] * (1 + len(near)),
        compiler_params=params,
        name="pack_near",
    )(panels, chip_q)
    messages = dict(zip(far + near, far_messages + near_messages, strict=True))

    received = [None] * slots
    for k in reversed(range(slots)):
        pairs = [
            (d, d ^ (2 * (2 * k + d % 2))) for d in range(devices) if 2 * k + d % 2
        ]
        received[k] = lax.ppermute(messages[k], "row", pairs)

    base = pl.pallas_call(
        local_kernel,
        out_shape=jax.ShapeDtypeStruct((chip_rows, columns), wide),
        in_specs=[VMEM()] * 3,
        out_specs=VMEM(),
        compiler_params=pltpu.CompilerParams(vmem_limit_bytes=32 * 2**20),
        name="local",
    )(panels[:chip_blocks], chip_q, local_rows)

    keep, send = pl.pallas_call(
        unpack_kernel,
        out_shape=[jax.ShapeDtypeStruct((rows, columns), wide)] * 2,
        in_specs=[VMEM()] * (2 + slots),
        out_specs=[VMEM()] * 2,
        scratch_shapes=[pltpu.VMEM((chip_rows, columns), wide)],
        compiler_params=pltpu.CompilerParams(vmem_limit_bytes=48 * 2**20),
        name="unpack",
    )(base, panels, *received)
    return (keep + swap(send)) * (1.0 / math.sqrt(rows * devices))


def solution(mesh):
    return jax.shard_map(
        functools.partial(on_device, mesh.shape["row"]),
        mesh=mesh,
        in_specs=(
            P(("grp", "row"), None, None),
            P(("grp", "row"), None),
            P(("grp", "row"), None),
            P(("grp", "row")),
        ),
        out_specs=P(("grp", "row"), None),
        check_vma=False,
    )
```

```python
import functools
import math

import jax
import jax.numpy as jnp
from jax import lax
from jax.experimental import pallas as pl
from jax.experimental.pallas import tpu as pltpu
from jax.sharding import PartitionSpec as P

TOP = 32700.0
STEPS = 16.0
LEAST = 1e-30


def place():
    me = lax.axis_index("row")
    return me // 2, me % 2


def scale_of(code):
    return jnp.exp2(code * (1.0 / STEPS))


def encode(x):
    top = jnp.maximum(jnp.max(jnp.abs(x), axis=0, keepdims=True), LEAST)
    code = jnp.ceil(jnp.log2(top) * STEPS)
    values = jnp.round(x * (TOP / scale_of(code)))
    return values.astype(jnp.int32).astype(jnp.int16), code


def put_tiles(index, count, tiles, panels, chip_blocks):
    chip, core = place()
    tile = tiles.shape[1]
    live = count[0]
    for r in range(1, count.shape[0]):
        live = live + count[r]

    def put(s, carry):
        i, j = index[0, s], index[1, s]
        cls = chip ^ (j // chip_blocks)

        @pl.when(cls % 2 == core)
        def _():
            panel = (cls // 2) * chip_blocks + j % chip_blocks
            at = pl.multiple_of((i % chip_blocks) * tile, tile)
            panels[panel, pl.ds(at, tile), :] = tiles[s]

        return carry

    lax.fori_loop(0, live, put, 0)


def own_kernel(index_ref, count_ref, tiles_ref, panels, index, count, tiles, sems):
    copies = [
        pltpu.make_async_copy(a, b, sems.at[n])
        for n, (a, b) in enumerate(
            ((index_ref, index), (count_ref, count), (tiles_ref, tiles))
        )
    ]
    for copy in copies:
        copy.start()
    panels[...] = jnp.zeros_like(panels)
    for copy in copies:
        copy.wait()
    put_tiles(index, count, tiles, panels, panels.shape[1] // panels.shape[2])


def write_message(message, blocks):
    tile = message.shape[1]
    codes = []
    for b, x in enumerate(blocks):
        values, code = encode(x)
        message[b * tile:(b + 1) * tile, :] = values
        codes.append(code)
    which = lax.broadcasted_iota(jnp.int32, (16, tile), 0)
    tail = jnp.zeros((16, tile), jnp.float32)
    for b, code in enumerate(codes):
        tail = jnp.where(which == b, code, tail)
    message[len(blocks) * tile:, :] = tail.astype(jnp.int32).astype(jnp.int16)


def read_message(message):
    tile = message.shape[1]
    blocks = message.shape[0] // tile
    tail = message[blocks * tile:, :].astype(jnp.int32).astype(jnp.float32)
    scales = scale_of(tail) * (1.0 / TOP)
    return [
        message[b * tile:(b + 1) * tile, :].astype(jnp.int32).astype(jnp.float32)
        * scales[b:b + 1, :]
        for b in range(blocks)
    ]


def mirrored_blocks(q_t, panels, slot):
    tile = panels.shape[2]
    chip_blocks = panels.shape[1] // tile
    blocks = []
    for g in range(slot * chip_blocks, (slot + 1) * chip_blocks, 2):
        pair = jnp.concatenate([panels[g], panels[g + 1]], axis=1)
        sums = jnp.dot(q_t, pair, preferred_element_type=jnp.float32)
        blocks += [sums[:, :tile], sums[:, tile:]]
    return blocks


def direct_sum(panels, slot, blocks):
    tile = panels.shape[2]
    chip_blocks = panels.shape[1] // tile
    total = None
    for b in range(0, chip_blocks, 2):
        g = slot * chip_blocks + b
        pair = jnp.concatenate([panels[g], panels[g + 1]], axis=1)
        q = jnp.concatenate(blocks[b:b + 2], axis=0).astype(jnp.bfloat16)
        part = jnp.dot(pair, q, preferred_element_type=jnp.float32)
        total = part if total is None else total + part
    return total


def split(x, tile):
    return [x[at:at + tile, :] for at in range(0, x.shape[0], tile)]


def in_lower_half(chips):
    return place()[0] < chips // 2


def far_kernel(
    chips, slots, index, count, tiles, own_q, other_q, _, panels, chip_q, *messages
):
    rows, tile = own_q.shape[0], panels.shape[2]
    _, core = place()
    chip_q[pl.ds(pl.multiple_of(core * rows, rows), rows), :] = own_q[...]
    chip_q[pl.ds(pl.multiple_of((1 - core) * rows, rows), rows), :] = other_q[...]

    @pl.when(in_lower_half(chips))
    def _():
        put_tiles(index, count, tiles, panels, panels.shape[1] // tile)
        q_t = chip_q[...].T
        for k, message in zip(slots, messages, strict=True):
            write_message(message, mirrored_blocks(q_t, panels, k))

    @pl.when(jnp.logical_not(in_lower_half(chips)))
    def _():
        write_message(messages[0], split(chip_q[...].astype(jnp.float32), tile))
        for message in messages[1:]:
            message[...] = messages[0][...]


def near_kernel(
    chips, slots, index, count, tiles, _, chip_q, panels, local_rows, *messages
):
    tile = panels.shape[2]
    chip, core = place()

    @pl.when(jnp.logical_not(in_lower_half(chips)))
    def _():
        put_tiles(index, count, tiles, panels, panels.shape[1] // tile)

    q = chip_q[...]
    q_t = q.T
    q_wide = q.astype(jnp.float32)
    for k, message in zip(slots, messages, strict=True):
        up = chip < (chip ^ (2 * k + core))
        blocks = mirrored_blocks(q_t, panels, k)
        if k == 0:
            for b, m in enumerate(blocks):
                local_rows[b * tile:(b + 1) * tile, :] = m
        write_message(
            message,
            [
                jnp.where(up, m, own)
                for m, own in zip(blocks, split(q_wide, tile), strict=True)
            ],
        )


def gather_part(slots, base, panels, received):
    tile = panels.shape[2]
    chip, core = place()
    total, mirrored = base
    for k, message in zip(slots, received, strict=True):
        low = (chip ^ (2 * k + core)) < chip
        blocks = read_message(message)
        mirrored = [
            m + jnp.where(low, x, 0.0) for m, x in zip(mirrored, blocks, strict=True)
        ]
        total = total + direct_sum(panels, k, blocks)
    return total, mirrored


def early_kernel(slots, panels, chip_q, local_rows, *refs):
    *received, direct, mirror = refs
    tile = panels.shape[2]
    _, core = place()
    total = direct_sum(panels, 0, split(chip_q[...], tile))
    base = (
        jnp.where(core == 0, total, 0.0),
        [jnp.where(core == 0, m, 0.0) for m in split(local_rows[...], tile)],
    )
    total, mirrored = gather_part(slots, base, panels, received)
    direct[...] = total
    for b, m in enumerate(mirrored):
        mirror[b * tile:(b + 1) * tile, :] = m


def late_kernel(slots, panels, direct, mirror, *refs):
    *received, keep, send, result = refs
    rows, tile = keep.shape[0], panels.shape[2]
    _, core = place()
    total, mirrored = gather_part(
        slots, (direct[...], split(mirror[...], tile)), panels, received
    )
    for b, (block, m) in enumerate(zip(split(total, tile), mirrored, strict=True)):
        result[b * tile:(b + 1) * tile, :] = block + m.T
    keep[...] = result[pl.ds(pl.multiple_of(core * rows, rows), rows), :]
    send[...] = result[pl.ds(pl.multiple_of((1 - core) * rows, rows), rows), :]


VMEM = functools.partial(pl.BlockSpec, memory_space=pltpu.VMEM)
SMEM = functools.partial(pl.BlockSpec, memory_space=pltpu.SMEM)


def on_device(devices, tile_blocks, q_block, tile_index, tile_count):
    tile = tile_blocks.shape[1]
    rows, columns = q_block.shape
    chips = devices // 2
    slots = chips // 2
    chip_rows = 2 * rows
    chip_blocks = chip_rows // tile
    wide = jnp.float32
    other_core = [(d, d ^ 1) for d in range(devices)]

    def swap(x):
        return lax.ppermute(x, "row", other_core)

    index = tile_index.T
    other_tiles = swap(tile_blocks)
    other_q = swap(q_block)
    other_index = swap(index)
    other_count = swap(tile_count)

    panels_shape = jax.ShapeDtypeStruct(
        (slots * chip_blocks, chip_rows, tile), jnp.bfloat16
    )
    q_shape = jax.ShapeDtypeStruct((chip_rows, columns), jnp.bfloat16)
    message = jax.ShapeDtypeStruct((chip_rows + 16, columns), jnp.int16)
    params = pltpu.CompilerParams(vmem_limit_bytes=48 * 2**20)
    own_panels = pl.pallas_call(
        own_kernel,
        out_shape=panels_shape,
        in_specs=[pl.BlockSpec(memory_space=pltpu.HBM)] * 3,
        out_specs=VMEM(),
        scratch_shapes=[
            pltpu.SMEM(index.shape, index.dtype),
            pltpu.SMEM(tile_count.shape, tile_count.dtype),
            pltpu.VMEM(tile_blocks.shape, tile_blocks.dtype),
            pltpu.SemaphoreType.DMA((3,)),
        ],
        compiler_params=params,
        name="own_tiles",
    )(*(pltpu.with_memory_space_constraint(a, pltpu.HBM) for a in (index, tile_count, tile_blocks)))
    far = list(range(slots // 2, slots))
    near = list(reversed(range(slots // 2)))
    wide_shape = jax.ShapeDtypeStruct((chip_rows, columns), wide)
    panels, chip_q, *far_messages = pl.pallas_call(
        functools.partial(far_kernel, chips, far),
        out_shape=[panels_shape, q_shape] + [message] * len(far),
        in_specs=[SMEM(), SMEM(), VMEM(), pl.BlockSpec(), VMEM(), VMEM()],
        out_specs=[VMEM()] * (2 + len(far)),
        input_output_aliases={5: 0},
        compiler_params=params,
        name="pack_far",
    )(other_index, other_count, other_tiles, q_block, other_q, own_panels)
    panels, local_rows, *near_messages = pl.pallas_call(
        functools.partial(near_kernel, chips, near),
        out_shape=[panels_shape, wide_shape] + [message] * len(near),
        in_specs=[SMEM(), SMEM()] + [VMEM()] * 3,
        out_specs=[VMEM()] * (2 + len(near)),
        input_output_aliases={3: 0},
        compiler_params=params,
        name="pack_near",
    )(other_index, other_count, other_tiles, panels, chip_q)
    messages = dict(zip(far + near, far_messages + near_messages, strict=True))
    received = {
        k: lax.ppermute(messages[k], "row", [
            (d, d ^ (2 * (2 * k + d % 2))) for d in range(devices) if 2 * k + d % 2
        ])
        for k in far + near
    }

    early = [far[0]]
    late = [k for k in far + near if k not in early]
    direct, mirror = pl.pallas_call(
        functools.partial(early_kernel, early),
        out_shape=[wide_shape] * 2,
        in_specs=[VMEM()] * (3 + len(early)),
        out_specs=[VMEM()] * 2,
        compiler_params=params,
        name="gather_early",
    )(panels, chip_q, local_rows, *(received[k] for k in early))
    keep, send = pl.pallas_call(
        functools.partial(late_kernel, late),
        out_shape=[jax.ShapeDtypeStruct((rows, columns), wide)] * 2,
        in_specs=[VMEM()] * (3 + len(late)),
        out_specs=[VMEM()] * 2,
        scratch_shapes=[pltpu.VMEM((chip_rows, columns), wide)],
        compiler_params=params,
        name="gather_late",
    )(panels, direct, mirror, *(received[k] for k in late))
    return (keep + swap(send)) * (1.0 / math.sqrt(rows * devices))


def solution(mesh):
    return jax.shard_map(
        functools.partial(on_device, mesh.shape["row"]),
        mesh=mesh,
        in_specs=(
            P(("grp", "row"), None, None),
            P(("grp", "row"), None),
            P(("grp", "row"), None),
            P(("grp", "row")),
        ),
        out_specs=P(("grp", "row"), None),
        check_vma=False,
    )
```

```python
import functools
import math

import jax
import jax.numpy as jnp
from jax import lax
from jax.experimental import pallas as pl
from jax.experimental.pallas import tpu as pltpu
from jax.sharding import PartitionSpec as P

TOP = 32700.0
STEPS = 16.0
LEAST = 1e-30


def place():
    me = lax.axis_index("row")
    return me // 2, me % 2


def scale_of(code):
    return jnp.exp2(code * (1.0 / STEPS))


def encode(x):
    top = jnp.maximum(jnp.max(jnp.abs(x), axis=0, keepdims=True), LEAST)
    code = jnp.ceil(jnp.log2(top) * STEPS)
    values = jnp.round(x * (TOP / scale_of(code)))
    return values.astype(jnp.int32).astype(jnp.int16), code


def live_tiles(count):
    live = count[0]
    for r in range(1, count.shape[0]):
        live = live + count[r]
    return live


def put_tiles(index, count, tiles, panels, chip_blocks):
    chip, core = place()
    tile = tiles.shape[1]
    local = panels.shape[0] // chip_blocks - 1
    live = live_tiles(count)

    def put(s, carry):
        i, j = index[0, s], index[1, s]
        cls = chip ^ (j // chip_blocks)

        @pl.when((cls == 0) | (cls % 2 == core))
        def _():
            slot = jnp.where(cls == 0, local, cls // 2)
            panel = slot * chip_blocks + j % chip_blocks
            at = pl.multiple_of((i % chip_blocks) * tile, tile)
            panels[panel, pl.ds(at, tile), :] = tiles[s]

        return carry

    lax.fori_loop(0, live, put, 0)


def fetch(sems, *pairs):
    copies = [
        pltpu.make_async_copy(a, b, sems.at[n]) for n, (a, b) in enumerate(pairs)
    ]
    for copy in copies:
        copy.start()
    return copies


def own_kernel(index_ref, count_ref, tiles_ref, panels, index, count, tiles, sems):
    copies = fetch(sems, (index_ref, index), (count_ref, count), (tiles_ref, tiles))
    panels[...] = jnp.zeros_like(panels)
    for copy in copies:
        copy.wait()
    put_tiles(index, count, tiles, panels, panels.shape[1] // panels.shape[2])


def direct_kernel(
    index_ref, count_ref, tiles_ref, panels, chip_q, rows_panels, direct, mirror,
    index, count, tiles, sems,
):
    copies = fetch(sems, (index_ref, index), (count_ref, count), (tiles_ref, tiles))
    rows_panels[...] = jnp.zeros_like(rows_panels)
    for copy in copies:
        copy.wait()
    tile = tiles.shape[1]
    rows = rows_panels.shape[1]
    chip_blocks = 2 * rows // tile
    chip, core = place()

    def put(s, carry):
        i, j = index[0, s], index[1, s]
        panel = (chip ^ (j // chip_blocks)) * chip_blocks + j % chip_blocks
        at = pl.multiple_of((i % (rows // tile)) * tile, tile)
        rows_panels[panel, pl.ds(at, tile), :] = tiles[s]
        return carry

    lax.fori_loop(0, live_tiles(count), put, 0)
    direct[...] = direct_sum(rows_panels, 0, split(chip_q[...], tile))
    q_t = chip_q[...].T
    local = panels.shape[0] - chip_blocks + core * (chip_blocks // 2)
    for b in range(rows // tile):
        mirror[b * tile:(b + 1) * tile, :] = jnp.dot(
            q_t, panels[local + b], preferred_element_type=jnp.float32
        )


def write_message(message, blocks):
    tile = message.shape[1]
    codes = []
    for b, x in enumerate(blocks):
        values, code = encode(x)
        message[b * tile:(b + 1) * tile, :] = values
        codes.append(code)
    which = lax.broadcasted_iota(jnp.int32, (16, tile), 0)
    tail = jnp.zeros((16, tile), jnp.float32)
    for b, code in enumerate(codes):
        tail = jnp.where(which == b, code, tail)
    message[len(blocks) * tile:, :] = tail.astype(jnp.int32).astype(jnp.int16)


def read_message(message):
    tile = message.shape[1]
    blocks = message.shape[0] // tile
    tail = message[blocks * tile:, :].astype(jnp.int32).astype(jnp.float32)
    scales = scale_of(tail) * (1.0 / TOP)
    return [
        message[b * tile:(b + 1) * tile, :].astype(jnp.int32).astype(jnp.float32)
        * scales[b:b + 1, :]
        for b in range(blocks)
    ]


def mirrored_blocks(q_t, panels, slot):
    tile = panels.shape[2]
    chip_blocks = panels.shape[1] // tile
    blocks = []
    for g in range(slot * chip_blocks, (slot + 1) * chip_blocks, 2):
        pair = jnp.concatenate([panels[g], panels[g + 1]], axis=1)
        sums = jnp.dot(q_t, pair, preferred_element_type=jnp.float32)
        blocks += [sums[:, :tile], sums[:, tile:]]
    return blocks


def direct_sum(panels, start, blocks):
    total = None
    for b in range(0, len(blocks), 2):
        pair = jnp.concatenate([panels[start + b], panels[start + b + 1]], axis=1)
        q = jnp.concatenate(blocks[b:b + 2], axis=0).astype(jnp.bfloat16)
        part = jnp.dot(pair, q, preferred_element_type=jnp.float32)
        total = part if total is None else total + part
    return total


def split(x, tile):
    return [x[at:at + tile, :] for at in range(0, x.shape[0], tile)]


def in_lower_half(chips):
    return place()[0] < chips // 2


def far_kernel(
    chips, slots, index_ref, count_ref, tiles, own_q, other_q, _, panels, chip_q, *refs
):
    *messages, index, count, sems = refs
    rows, tile = own_q.shape[0], panels.shape[2]
    _, core = place()
    chip_q[pl.ds(pl.multiple_of(core * rows, rows), rows), :] = own_q[...]
    chip_q[pl.ds(pl.multiple_of((1 - core) * rows, rows), rows), :] = other_q[...]

    @pl.when(in_lower_half(chips))
    def _():
        for copy in fetch(sems, (index_ref, index), (count_ref, count)):
            copy.wait()
        put_tiles(index, count, tiles, panels, panels.shape[1] // tile)
        q_t = chip_q[...].T
        for k, message in zip(slots, messages, strict=True):
            write_message(message, mirrored_blocks(q_t, panels, k))

    @pl.when(jnp.logical_not(in_lower_half(chips)))
    def _():
        write_message(messages[0], split(chip_q[...].astype(jnp.float32), tile))
        for message in messages[1:]:
            message[...] = messages[0][...]


def near_kernel(
    chips, slots, index, count, tiles, _, chip_q, panels, *messages
):
    tile = panels.shape[2]
    chip, core = place()

    @pl.when(jnp.logical_not(in_lower_half(chips)))
    def _():
        put_tiles(index, count, tiles, panels, panels.shape[1] // tile)

    q = chip_q[...]
    q_t = q.T
    q_wide = q.astype(jnp.float32)
    for k, message in zip(slots, messages, strict=True):
        up = chip < (chip ^ (2 * k + core))
        blocks = mirrored_blocks(q_t, panels, k)
        write_message(
            message,
            [
                jnp.where(up, m, own)
                for m, own in zip(blocks, split(q_wide, tile), strict=True)
            ],
        )


def gather_part(sources, rows_panels, direct, mirror, messages):
    tile = rows_panels.shape[2]
    chip, core = place()
    total = direct[...]
    mirrored = split(mirror[...], tile)
    half = len(mirrored)
    for (k, mine), message in zip(sources, messages, strict=True):
        cls = 2 * k + (core if mine else 1 - core)
        low = (chip ^ cls) < chip
        blocks = read_message(message)
        total = total + direct_sum(rows_panels, cls * 2 * half, blocks)
        mirrored = [
            m + jnp.where(low, jnp.where(core == 0, a, b), 0.0)
            for m, a, b in zip(mirrored, blocks[:half], blocks[half:], strict=True)
        ]
    return total, mirrored


def gather_kernel(sources, rows_panels, direct, mirror, *refs):
    *messages, direct_out, mirror_out = refs
    tile = rows_panels.shape[2]
    total, mirrored = gather_part(sources, rows_panels, direct, mirror, messages)
    direct_out[...] = total
    for b, m in enumerate(mirrored):
        mirror_out[b * tile:(b + 1) * tile, :] = m


def final_kernel(sources, factor, rows_panels, direct, mirror, *refs):
    *messages, out, result, sems = refs
    tile = rows_panels.shape[2]
    total, mirrored = gather_part(sources, rows_panels, direct, mirror, messages)
    copies = []
    for b, (block, m) in enumerate(zip(split(total, tile), mirrored, strict=True)):
        at = pl.ds(b * tile, tile)
        result[at, :] = (block + m.T) * factor
        copies.append(pltpu.make_async_copy(result.at[at], out.at[at], sems.at[b]))
        copies[-1].start()
    for copy in copies:
        copy.wait()


VMEM = functools.partial(pl.BlockSpec, memory_space=pltpu.VMEM)
SMEM = functools.partial(pl.BlockSpec, memory_space=pltpu.SMEM)


def on_device(devices, tile_blocks, q_block, tile_index, tile_count):
    tile = tile_blocks.shape[1]
    rows, columns = q_block.shape
    chips = devices // 2
    slots = chips // 2
    chip_rows = 2 * rows
    chip_blocks = chip_rows // tile
    wide = jnp.float32
    other_core = [(d, d ^ 1) for d in range(devices)]

    def swap(x):
        return lax.ppermute(x, "row", other_core)

    index = tile_index.T
    other_tiles = swap(tile_blocks)
    other_q = swap(q_block)
    other_index = swap(index)
    other_count = swap(tile_count)

    panels_shape = jax.ShapeDtypeStruct(
        ((slots + 1) * chip_blocks, chip_rows, tile), jnp.bfloat16
    )
    rows_panels_shape = jax.ShapeDtypeStruct(
        (chips * chip_blocks, rows, tile), jnp.bfloat16
    )
    q_shape = jax.ShapeDtypeStruct((chip_rows, columns), jnp.bfloat16)
    message = jax.ShapeDtypeStruct((chip_rows + 16, columns), jnp.int16)
    half_shape = jax.ShapeDtypeStruct((rows, columns), wide)
    params = pltpu.CompilerParams(vmem_limit_bytes=48 * 2**20)
    hbm = pl.BlockSpec(memory_space=pltpu.HBM)
    own = [
        pltpu.with_memory_space_constraint(a, pltpu.HBM)
        for a in (index, tile_count, tile_blocks)
    ]
    own_scratch = [
        pltpu.SMEM(index.shape, index.dtype),
        pltpu.SMEM(tile_count.shape, tile_count.dtype),
        pltpu.VMEM(tile_blocks.shape, tile_blocks.dtype),
        pltpu.SemaphoreType.DMA((3,)),
    ]
    own_panels = pl.pallas_call(
        own_kernel,
        out_shape=panels_shape,
        in_specs=[hbm] * 3,
        out_specs=VMEM(),
        scratch_shapes=own_scratch,
        compiler_params=params,
        name="own_tiles",
    )(*own)
    far = list(range(slots // 2, slots))
    near = list(reversed(range(slots // 2)))
    panels, chip_q, *far_messages = pl.pallas_call(
        functools.partial(far_kernel, chips, far),
        out_shape=[panels_shape, q_shape] + [message] * len(far),
        in_specs=[pl.BlockSpec(memory_space=pl.ANY)] * 2 + [VMEM()] * 4,
        out_specs=[VMEM()] * (2 + len(far)),
        scratch_shapes=own_scratch[:2] + [pltpu.SemaphoreType.DMA((2,))],
        input_output_aliases={5: 0},
        compiler_params=params,
        name="pack_far",
    )(other_index, other_count, other_tiles, q_block, other_q, own_panels)
    panels, *near_messages = pl.pallas_call(
        functools.partial(near_kernel, chips, near),
        out_shape=[panels_shape] + [message] * len(near),
        in_specs=[SMEM(), SMEM()] + [VMEM()] * 3,
        out_specs=[VMEM()] * (1 + len(near)),
        input_output_aliases={3: 0},
        compiler_params=params,
        name="pack_near",
    )(other_index, other_count, other_tiles, panels, chip_q)
    messages = dict(zip(far + near, far_messages + near_messages, strict=True))
    received = {
        k: lax.ppermute(messages[k], "row", [
            (d, d ^ (2 * (2 * k + d % 2))) for d in range(devices) if 2 * k + d % 2
        ])
        for k in far + near
    }

    rows_panels, direct, mirror = pl.pallas_call(
        direct_kernel,
        out_shape=[rows_panels_shape, half_shape, half_shape],
        in_specs=[hbm] * 3 + [VMEM()] * 2,
        out_specs=[VMEM()] * 3,
        scratch_shapes=own_scratch,
        compiler_params=params,
        cost_estimate=pl.CostEstimate(flops=10000000000, bytes_accessed=0, transcendentals=0),
            name="direct_local",
    )(*own, panels, chip_q)

    other = {k: swap(received[k]) for k in received}

    def gather(sources, direct, mirror, name):
        return pl.pallas_call(
            functools.partial(gather_kernel, sources),
            out_shape=[half_shape] * 2,
            in_specs=[VMEM()] * (3 + len(sources)),
            out_specs=[VMEM()] * 2,
            compiler_params=params,
            cost_estimate=pl.CostEstimate(
                flops=10**10, bytes_accessed=0, transcendentals=0
            ),
            name=name,
        )(rows_panels, direct, mirror,
          *((received if mine else other)[k] for k, mine in sources))

    *late, last = near + far[1:]
    sums = gather([(far[0], True), (far[0], False)], direct, mirror, "gather_first")
    sums = gather([(k, mine) for k in late for mine in (True, False)], *sums, "gather_near")
    sums = gather([(last, True)], *sums, "gather_own")
    return pl.pallas_call(
        functools.partial(
            final_kernel, [(last, False)], 1.0 / math.sqrt(rows * devices)
        ),
        out_shape=half_shape,
        in_specs=[VMEM()] * 4,
        out_specs=hbm,
        scratch_shapes=[
            pltpu.VMEM((rows, columns), wide),
            pltpu.SemaphoreType.DMA((rows // tile,)),
        ],
        compiler_params=params,
        name="gather_last",
    )(rows_panels, *sums, other[last])


def solution(mesh):
    return jax.shard_map(
        functools.partial(on_device, mesh.shape["row"]),
        mesh=mesh,
        in_specs=(
            P(("grp", "row"), None, None),
            P(("grp", "row"), None),
            P(("grp", "row"), None),
            P(("grp", "row")),
        ),
        out_specs=P(("grp", "row"), None),
        check_vma=False,
    )
```

```python
import functools
import math

import jax
import jax.numpy as jnp
from jax import lax
from jax.experimental import pallas as pl
from jax.experimental.pallas import tpu as pltpu
from jax.sharding import PartitionSpec as P

TOP = 32700.0
STEPS = 16.0
LEAST = 1e-30


def place():
    me = lax.axis_index("row")
    return me // 2, me % 2


def scale_of(code):
    return jnp.exp2(code * (1.0 / STEPS))


def encode(x):
    top = jnp.maximum(jnp.max(jnp.abs(x), axis=0, keepdims=True), LEAST)
    code = jnp.ceil(jnp.log2(top) * STEPS)
    values = jnp.round(x * (TOP / scale_of(code)))
    return values.astype(jnp.int32).astype(jnp.int16), code


def live_tiles(count):
    live = count[0]
    for r in range(1, count.shape[0]):
        live = live + count[r]
    return live


def put_tiles(index, count, tiles, panels, chip_blocks):
    chip, core = place()
    tile = tiles.shape[1]
    local = panels.shape[0] // chip_blocks - 1
    live = live_tiles(count)

    def put(s, carry):
        i, j = index[0, s], index[1, s]
        cls = chip ^ (j // chip_blocks)

        @pl.when((cls == 0) | (cls % 2 == core))
        def _():
            slot = jnp.where(cls == 0, local, cls // 2)
            panel = slot * chip_blocks + j % chip_blocks
            at = pl.multiple_of((i % chip_blocks) * tile, tile)
            panels[panel, pl.ds(at, tile), :] = tiles[s]

        return carry

    lax.fori_loop(0, live, put, 0)


def fetch(sems, *pairs):
    copies = [
        pltpu.make_async_copy(a, b, sems.at[n]) for n, (a, b) in enumerate(pairs)
    ]
    for copy in copies:
        copy.start()
    return copies


def own_kernel(index_ref, count_ref, tiles_ref, panels, index, count, tiles, sems):
    copies = fetch(sems, (index_ref, index), (count_ref, count), (tiles_ref, tiles))
    panels[...] = jnp.zeros_like(panels)
    for copy in copies:
        copy.wait()
    put_tiles(index, count, tiles, panels, panels.shape[1] // panels.shape[2])


def direct_kernel(
    index_ref, count_ref, tiles_ref, panels, chip_q, rows_panels, direct, mirror,
    index, count, tiles, sems,
):
    copies = fetch(sems, (index_ref, index), (count_ref, count), (tiles_ref, tiles))
    rows_panels[...] = jnp.zeros_like(rows_panels)
    for copy in copies:
        copy.wait()
    tile = tiles.shape[1]
    rows = rows_panels.shape[1]
    chip_blocks = 2 * rows // tile
    chip, core = place()

    def put(s, carry):
        i, j = index[0, s], index[1, s]
        panel = (chip ^ (j // chip_blocks)) * chip_blocks + j % chip_blocks
        at = pl.multiple_of((i % (rows // tile)) * tile, tile)
        rows_panels[panel, pl.ds(at, tile), :] = tiles[s]
        return carry

    lax.fori_loop(0, live_tiles(count), put, 0)
    direct[...] = direct_sum(rows_panels, 0, split(chip_q[...], tile))
    q_t = chip_q[...].T
    local = panels.shape[0] - chip_blocks + core * (chip_blocks // 2)
    for b in range(rows // tile):
        mirror[b * tile:(b + 1) * tile, :] = jnp.dot(
            q_t, panels[local + b], preferred_element_type=jnp.float32
        )


def write_message(message, blocks):
    tile = message.shape[1]
    codes = []
    for b, x in enumerate(blocks):
        values, code = encode(x)
        message[b * tile:(b + 1) * tile, :] = values
        codes.append(code)
    which = lax.broadcasted_iota(jnp.int32, (16, tile), 0)
    tail = jnp.zeros((16, tile), jnp.float32)
    for b, code in enumerate(codes):
        tail = jnp.where(which == b, code, tail)
    message[len(blocks) * tile:, :] = tail.astype(jnp.int32).astype(jnp.int16)


def read_message(message):
    tile = message.shape[1]
    blocks = message.shape[0] // tile
    tail = message[blocks * tile:, :].astype(jnp.int32).astype(jnp.float32)
    scales = scale_of(tail) * (1.0 / TOP)
    return [
        message[b * tile:(b + 1) * tile, :].astype(jnp.int32).astype(jnp.float32)
        * scales[b:b + 1, :]
        for b in range(blocks)
    ]


def mirrored_blocks(q_t, panels, slot):
    tile = panels.shape[2]
    chip_blocks = panels.shape[1] // tile
    blocks = []
    for g in range(slot * chip_blocks, (slot + 1) * chip_blocks, 2):
        pair = jnp.concatenate([panels[g], panels[g + 1]], axis=1)
        sums = jnp.dot(q_t, pair, preferred_element_type=jnp.float32)
        blocks += [sums[:, :tile], sums[:, tile:]]
    return blocks


def direct_sum(panels, start, blocks):
    total = None
    for b in range(0, len(blocks), 2):
        pair = jnp.concatenate([panels[start + b], panels[start + b + 1]], axis=1)
        q = jnp.concatenate(blocks[b:b + 2], axis=0).astype(jnp.bfloat16)
        part = jnp.dot(pair, q, preferred_element_type=jnp.float32)
        total = part if total is None else total + part
    return total


def split(x, tile):
    return [x[at:at + tile, :] for at in range(0, x.shape[0], tile)]


def in_lower_half(chips):
    return place()[0] < chips // 2


def far_kernel(
    chips, slots, index_ref, count_ref, tiles, own_q, other_q, _, panels, chip_q, *refs
):
    *messages, index, count, sems = refs
    rows, tile = own_q.shape[0], panels.shape[2]
    _, core = place()
    chip_q[pl.ds(pl.multiple_of(core * rows, rows), rows), :] = own_q[...]
    chip_q[pl.ds(pl.multiple_of((1 - core) * rows, rows), rows), :] = other_q[...]

    @pl.when(in_lower_half(chips))
    def _():
        copies = fetch(sems, (index_ref, index), (count_ref, count))
        q_t = chip_q[...].T
        for copy in copies:
            copy.wait()
        put_tiles(index, count, tiles, panels, panels.shape[1] // tile)
        for k, message in zip(slots, messages, strict=True):
            write_message(message, mirrored_blocks(q_t, panels, k))

    @pl.when(jnp.logical_not(in_lower_half(chips)))
    def _():
        write_message(messages[0], split(chip_q[...].astype(jnp.float32), tile))
        for message in messages[1:]:
            message[...] = messages[0][...]


def near_kernel(
    chips, slots, index_ref, count_ref, tiles, _, chip_q, panels, *refs
):
    *messages, index, count, sems = refs
    tile = panels.shape[2]
    chip, core = place()
    q = chip_q[...]

    @pl.when(jnp.logical_not(in_lower_half(chips)))
    def _():
        for copy in fetch(sems, (index_ref, index), (count_ref, count)):
            copy.wait()
        put_tiles(index, count, tiles, panels, panels.shape[1] // tile)

    q_t = q.T
    q_wide = q.astype(jnp.float32)
    for k, message in zip(slots, messages, strict=True):
        up = chip < (chip ^ (2 * k + core))
        write_message(
            message,
            [
                jnp.where(up, m, own)
                for m, own in zip(
                    mirrored_blocks(q_t, panels, k), split(q_wide, tile), strict=True
                )
            ],
        )


def gather_part(sources, rows_panels, direct, mirror, messages):
    tile = rows_panels.shape[2]
    chip, core = place()
    total = direct[...]
    mirrored = split(mirror[...], tile)
    half = len(mirrored)
    for (k, mine), message in zip(sources, messages, strict=True):
        cls = 2 * k + (core if mine else 1 - core)
        low = (chip ^ cls) < chip
        blocks = read_message(message)
        total = total + direct_sum(rows_panels, cls * 2 * half, blocks)
        mirrored = [
            m + jnp.where(low, jnp.where(core == 0, a, b), 0.0)
            for m, a, b in zip(mirrored, blocks[:half], blocks[half:], strict=True)
        ]
    return total, mirrored


def gather_kernel(sources, rows_panels, direct, mirror, *refs):
    *messages, direct_out, mirror_out = refs
    tile = rows_panels.shape[2]
    total, mirrored = gather_part(sources, rows_panels, direct, mirror, messages)
    direct_out[...] = total
    for b, m in enumerate(mirrored):
        mirror_out[b * tile:(b + 1) * tile, :] = m


def final_kernel(sources, factor, rows_panels, direct, mirror, *refs):
    *messages, out, result, sems = refs
    tile = rows_panels.shape[2]
    total, mirrored = gather_part(sources, rows_panels, direct, mirror, messages)
    copies = []
    for b, (block, m) in enumerate(zip(split(total, tile), mirrored, strict=True)):
        at = pl.ds(b * tile, tile)
        result[at, :] = (block + m.T) * factor
        copies.append(pltpu.make_async_copy(result.at[at], out.at[at], sems.at[b]))
        copies[-1].start()
    for copy in copies:
        copy.wait()


VMEM = functools.partial(pl.BlockSpec, memory_space=pltpu.VMEM)
SMEM = functools.partial(pl.BlockSpec, memory_space=pltpu.SMEM)


def on_device(devices, tile_blocks, q_block, tile_index, tile_count):
    tile = tile_blocks.shape[1]
    rows, columns = q_block.shape
    chips = devices // 2
    slots = chips // 2
    chip_rows = 2 * rows
    chip_blocks = chip_rows // tile
    wide = jnp.float32
    other_core = [(d, d ^ 1) for d in range(devices)]

    def swap(x):
        return lax.ppermute(x, "row", other_core)

    index = tile_index.T
    other_tiles = swap(tile_blocks)
    other_q = swap(q_block)
    other_index = swap(index)
    other_count = swap(tile_count)

    panels_shape = jax.ShapeDtypeStruct(
        ((slots + 1) * chip_blocks, chip_rows, tile), jnp.bfloat16
    )
    rows_panels_shape = jax.ShapeDtypeStruct(
        (chips * chip_blocks, rows, tile), jnp.bfloat16
    )
    q_shape = jax.ShapeDtypeStruct((chip_rows, columns), jnp.bfloat16)
    message = jax.ShapeDtypeStruct((chip_rows + 16, columns), jnp.int16)
    half_shape = jax.ShapeDtypeStruct((rows, columns), wide)
    params = pltpu.CompilerParams(vmem_limit_bytes=48 * 2**20)
    hbm = pl.BlockSpec(memory_space=pltpu.HBM)
    own = [
        pltpu.with_memory_space_constraint(a, pltpu.HBM)
        for a in (index, tile_count, tile_blocks)
    ]
    own_scratch = [
        pltpu.SMEM(index.shape, index.dtype),
        pltpu.SMEM(tile_count.shape, tile_count.dtype),
        pltpu.VMEM(tile_blocks.shape, tile_blocks.dtype),
        pltpu.SemaphoreType.DMA((3,)),
    ]
    own_panels = pl.pallas_call(
        own_kernel,
        out_shape=panels_shape,
        in_specs=[hbm] * 3,
        out_specs=VMEM(),
        scratch_shapes=own_scratch,
        compiler_params=params,
        name="own_tiles",
    )(*own)
    far = list(range(slots // 2, slots))
    near = list(reversed(range(slots // 2)))
    rest = near + far[1:]
    first = far[:1]
    panels, chip_q, *far_messages = pl.pallas_call(
        functools.partial(far_kernel, chips, first),
        out_shape=[panels_shape, q_shape] + [message] * len(first),
        in_specs=[pl.BlockSpec(memory_space=pl.ANY)] * 2 + [VMEM()] * 4,
        out_specs=[VMEM()] * (2 + len(first)),
        scratch_shapes=own_scratch[:2] + [pltpu.SemaphoreType.DMA((2,))],
        input_output_aliases={5: 0},
        compiler_params=params,
        name="pack_far",
    )(other_index, other_count, other_tiles, q_block, other_q, own_panels)
    panels, *rest_messages = pl.pallas_call(
        functools.partial(near_kernel, chips, rest),
        out_shape=[panels_shape] + [message] * len(rest),
        in_specs=[pl.BlockSpec(memory_space=pl.ANY)] * 2 + [VMEM()] * 3,
        out_specs=[VMEM()] * (1 + len(rest)),
        scratch_shapes=own_scratch[:2] + [pltpu.SemaphoreType.DMA((2,))],
        input_output_aliases={3: 0},
        compiler_params=params,
        name="pack_near",
    )(other_index, other_count, other_tiles, panels, chip_q)
    messages = dict(zip(first + rest, far_messages + rest_messages, strict=True))
    received = {
        k: lax.ppermute(messages[k], "row", [
            (d, d ^ (2 * (2 * k + d % 2))) for d in range(devices) if 2 * k + d % 2
        ])
        for k in first + rest
    }

    rows_panels, direct, mirror = pl.pallas_call(
        direct_kernel,
        out_shape=[rows_panels_shape, half_shape, half_shape],
        in_specs=[hbm] * 3 + [VMEM()] * 2,
        out_specs=[VMEM()] * 3,
        scratch_shapes=own_scratch,
        compiler_params=params,
        cost_estimate=pl.CostEstimate(flops=10000000000, bytes_accessed=0, transcendentals=0),
            name="direct_local",
    )(*own, panels, chip_q)

    other = {k: swap(received[k]) for k in received}

    def gather(sources, direct, mirror, name):
        return pl.pallas_call(
            functools.partial(gather_kernel, sources),
            out_shape=[half_shape] * 2,
            in_specs=[VMEM()] * (3 + len(sources)),
            out_specs=[VMEM()] * 2,
            compiler_params=params,
            cost_estimate=pl.CostEstimate(
                flops=10**10, bytes_accessed=0, transcendentals=0
            ),
            name=name,
        )(rows_panels, direct, mirror,
          *((received if mine else other)[k] for k, mine in sources))

    *late, last = near + far[1:]
    sums = gather([(far[0], True), (far[0], False)], direct, mirror, "gather_first")
    sums = gather([(k, mine) for k in late for mine in (True, False)], *sums, "gather_near")
    sums = gather([(last, True)], *sums, "gather_own")
    return pl.pallas_call(
        functools.partial(
            final_kernel, [(last, False)], 1.0 / math.sqrt(rows * devices)
        ),
        out_shape=half_shape,
        in_specs=[VMEM()] * 4,
        out_specs=hbm,
        scratch_shapes=[
            pltpu.VMEM((rows, columns), wide),
            pltpu.SemaphoreType.DMA((rows // tile,)),
        ],
        compiler_params=params,
        name="gather_last",
    )(rows_panels, *sums, other[last])


def solution(mesh):
    return jax.shard_map(
        functools.partial(on_device, mesh.shape["row"]),
        mesh=mesh,
        in_specs=(
            P(("grp", "row"), None, None),
            P(("grp", "row"), None),
            P(("grp", "row"), None),
            P(("grp", "row")),
        ),
        out_specs=P(("grp", "row"), None),
        check_vma=False,
    )
```

```python
import functools
import math

import jax
import jax.numpy as jnp
from jax import lax
from jax.experimental import pallas as pl
from jax.experimental.pallas import tpu as pltpu
from jax.sharding import PartitionSpec as P

TOP = 32700.0
STEPS = 16.0
LEAST = 1e-30


def place():
    me = lax.axis_index("row")
    return me // 2, me % 2


def scale_of(code):
    return jnp.exp2(code * (1.0 / STEPS))


def encode(x):
    top = jnp.maximum(jnp.max(jnp.abs(x), axis=0, keepdims=True), LEAST)
    code = jnp.ceil(jnp.log2(top) * STEPS)
    values = jnp.round(x * (TOP / scale_of(code)))
    return values.astype(jnp.int32).astype(jnp.int16), code


def live_tiles(count):
    live = count[0]
    for r in range(1, count.shape[0]):
        live = live + count[r]
    return live


def put_tiles(index, count, tiles, panels, chip_blocks):
    chip, core = place()
    tile = tiles.shape[1]
    local = panels.shape[0] // chip_blocks - 1
    live = live_tiles(count)

    def put(s, carry):
        i, j = index[0, s], index[1, s]
        cls = chip ^ (j // chip_blocks)

        @pl.when((cls == 0) | (cls % 2 == core))
        def _():
            slot = jnp.where(cls == 0, local, cls // 2)
            panel = slot * chip_blocks + j % chip_blocks
            at = pl.multiple_of((i % chip_blocks) * tile, tile)
            panels[panel, pl.ds(at, tile), :] = tiles[s]

        return carry

    lax.fori_loop(0, live, put, 0)


def fetch(sems, *pairs):
    copies = [
        pltpu.make_async_copy(a, b, sems.at[n]) for n, (a, b) in enumerate(pairs)
    ]
    for copy in copies:
        copy.start()
    return copies


def own_kernel(index_ref, count_ref, tiles_ref, panels, index, count, tiles, sems):
    copies = fetch(sems, (index_ref, index), (count_ref, count), (tiles_ref, tiles))
    panels[...] = jnp.zeros_like(panels)
    for copy in copies:
        copy.wait()
    put_tiles(index, count, tiles, panels, panels.shape[1] // panels.shape[2])


def direct_kernel(
    index_ref, count_ref, tiles_ref, panels, chip_q, rows_panels, direct, mirror,
    index, count, tiles, sems,
):
    copies = fetch(sems, (index_ref, index), (count_ref, count), (tiles_ref, tiles))
    rows_panels[...] = jnp.zeros_like(rows_panels)
    for copy in copies:
        copy.wait()
    tile = tiles.shape[1]
    rows = rows_panels.shape[1]
    chip_blocks = 2 * rows // tile
    chip, core = place()

    def put(s, carry):
        i, j = index[0, s], index[1, s]
        panel = (chip ^ (j // chip_blocks)) * chip_blocks + j % chip_blocks
        at = pl.multiple_of((i % (rows // tile)) * tile, tile)
        rows_panels[panel, pl.ds(at, tile), :] = tiles[s]
        return carry

    lax.fori_loop(0, live_tiles(count), put, 0)
    direct[...] = direct_sum(rows_panels, 0, split(chip_q[...], tile))
    q_t = chip_q[...].T
    local = panels.shape[0] - chip_blocks + core * (chip_blocks // 2)
    for b in range(rows // tile):
        mirror[b * tile:(b + 1) * tile, :] = jnp.dot(
            q_t, panels[local + b], preferred_element_type=jnp.float32
        )


def write_message(message, blocks):
    tile = message.shape[1]
    codes = []
    for b, x in enumerate(blocks):
        values, code = encode(x)
        message[b * tile:(b + 1) * tile, :] = values
        codes.append(code)
    which = lax.broadcasted_iota(jnp.int32, (16, tile), 0)
    tail = jnp.zeros((16, tile), jnp.float32)
    for b, code in enumerate(codes):
        tail = jnp.where(which == b, code, tail)
    message[len(blocks) * tile:, :] = tail.astype(jnp.int32).astype(jnp.int16)


def read_message(message):
    tile = message.shape[1]
    blocks = message.shape[0] // tile
    tail = message[blocks * tile:, :].astype(jnp.int32).astype(jnp.float32)
    scales = scale_of(tail) * (1.0 / TOP)
    return [
        message[b * tile:(b + 1) * tile, :].astype(jnp.int32).astype(jnp.float32)
        * scales[b:b + 1, :]
        for b in range(blocks)
    ]


def mirrored_blocks(q_t, panels, slot):
    tile = panels.shape[2]
    chip_blocks = panels.shape[1] // tile
    blocks = []
    for g in range(slot * chip_blocks, (slot + 1) * chip_blocks, 2):
        pair = jnp.concatenate([panels[g], panels[g + 1]], axis=1)
        sums = jnp.dot(q_t, pair, preferred_element_type=jnp.float32)
        blocks += [sums[:, :tile], sums[:, tile:]]
    return blocks


def direct_sum(panels, start, blocks):
    total = None
    for b in range(0, len(blocks), 2):
        pair = jnp.concatenate([panels[start + b], panels[start + b + 1]], axis=1)
        q = jnp.concatenate(blocks[b:b + 2], axis=0).astype(jnp.bfloat16)
        part = jnp.dot(pair, q, preferred_element_type=jnp.float32)
        total = part if total is None else total + part
    return total


def split(x, tile):
    return [x[at:at + tile, :] for at in range(0, x.shape[0], tile)]


def in_lower_half(chips):
    return place()[0] < chips // 2


def far_kernel(
    chips, slots, index_ref, count_ref, tiles, own_q, other_q, _, panels, chip_q, *refs
):
    *messages, index, count, sems = refs
    rows, tile = own_q.shape[0], panels.shape[2]
    _, core = place()
    chip_q[pl.ds(pl.multiple_of(core * rows, rows), rows), :] = own_q[...]
    chip_q[pl.ds(pl.multiple_of((1 - core) * rows, rows), rows), :] = other_q[...]

    @pl.when(in_lower_half(chips))
    def _():
        copies = fetch(sems, (index_ref, index), (count_ref, count))
        q_t = chip_q[...].T
        for copy in copies:
            copy.wait()
        put_tiles(index, count, tiles, panels, panels.shape[1] // tile)
        for k, message in zip(slots, messages, strict=True):
            write_message(message, mirrored_blocks(q_t, panels, k))

    @pl.when(jnp.logical_not(in_lower_half(chips)))
    def _():
        write_message(messages[0], split(chip_q[...].astype(jnp.float32), tile))
        for message in messages[1:]:
            message[...] = messages[0][...]


def near_kernel(
    chips, slots, index_ref, count_ref, tiles, _, chip_q, panels, *refs
):
    *messages, index, count, sems = refs
    tile = panels.shape[2]
    chip, core = place()
    q = chip_q[...]

    @pl.when(jnp.logical_not(in_lower_half(chips)))
    def _():
        for copy in fetch(sems, (index_ref, index), (count_ref, count)):
            copy.wait()
        put_tiles(index, count, tiles, panels, panels.shape[1] // tile)

    q_t = q.T
    q_wide = q.astype(jnp.float32)
    for k, message in zip(slots, messages, strict=True):
        up = chip < (chip ^ (2 * k + core))
        write_message(
            message,
            [
                jnp.where(up, m, own)
                for m, own in zip(
                    mirrored_blocks(q_t, panels, k), split(q_wide, tile), strict=True
                )
            ],
        )


def is_low(k, mine):
    chip, core = place()
    cls = 2 * k + (core if mine else 1 - core)
    return (chip ^ cls) < chip, cls


def own_half(blocks):
    _, core = place()
    half = len(blocks) // 2
    return [
        jnp.where(core == 0, a, b)
        for a, b in zip(blocks[:half], blocks[half:], strict=True)
    ]


def gather_part(sources, rows_panels, direct, mirror, messages):
    total = direct[...]
    mirrored = split(mirror[...], rows_panels.shape[2])
    for (k, mine), message in zip(sources, messages, strict=True):
        low, cls = is_low(k, mine)
        blocks = read_message(message)
        total = total + direct_sum(rows_panels, cls * len(blocks), blocks)
        mirrored = [
            m + jnp.where(low, x, 0.0)
            for m, x in zip(mirrored, own_half(blocks), strict=True)
        ]
    return total, mirrored


def gather_kernel(sources, rows_panels, direct, mirror, *refs):
    *messages, direct_out, mirror_out = refs
    tile = rows_panels.shape[2]
    total, mirrored = gather_part(sources, rows_panels, direct, mirror, messages)
    direct_out[...] = total
    for b, m in enumerate(mirrored):
        mirror_out[b * tile:(b + 1) * tile, :] = m


def join_kernel(sources, rows_panels, direct, mirror, *refs):
    *messages, base = refs
    tile = rows_panels.shape[2]
    total, mirrored = gather_part(sources, rows_panels, direct, mirror, messages)
    for b, (block, m) in enumerate(zip(split(total, tile), mirrored, strict=True)):
        base[b * tile:(b + 1) * tile, :] = block + m.T


def final_kernel(k, factor, rows_panels, base, message, out, result, sem):
    tile = rows_panels.shape[2]
    low, cls = is_low(k, False)

    @pl.when(low)
    def _():
        for b, x in enumerate(own_half(read_message(message))):
            at = slice(b * tile, (b + 1) * tile)
            result[at, :] = (base[at, :] + x.T) * factor

    @pl.when(jnp.logical_not(low))
    def _():
        blocks = read_message(message)
        total = direct_sum(rows_panels, cls * len(blocks), blocks)
        result[...] = (base[...] + total) * factor

    copy = pltpu.make_async_copy(result, out, sem)
    copy.start()
    copy.wait()


VMEM = functools.partial(pl.BlockSpec, memory_space=pltpu.VMEM)
SMEM = functools.partial(pl.BlockSpec, memory_space=pltpu.SMEM)


def on_device(devices, tile_blocks, q_block, tile_index, tile_count):
    tile = tile_blocks.shape[1]
    rows, columns = q_block.shape
    chips = devices // 2
    slots = chips // 2
    chip_rows = 2 * rows
    chip_blocks = chip_rows // tile
    wide = jnp.float32
    other_core = [(d, d ^ 1) for d in range(devices)]

    def swap(x):
        return lax.ppermute(x, "row", other_core)

    index = tile_index.T
    other_tiles = swap(tile_blocks)
    other_q = swap(q_block)
    other_index = swap(index)
    other_count = swap(tile_count)

    panels_shape = jax.ShapeDtypeStruct(
        ((slots + 1) * chip_blocks, chip_rows, tile), jnp.bfloat16
    )
    rows_panels_shape = jax.ShapeDtypeStruct(
        (chips * chip_blocks, rows, tile), jnp.bfloat16
    )
    q_shape = jax.ShapeDtypeStruct((chip_rows, columns), jnp.bfloat16)
    message = jax.ShapeDtypeStruct((chip_rows + 16, columns), jnp.int16)
    half_shape = jax.ShapeDtypeStruct((rows, columns), wide)
    params = pltpu.CompilerParams(vmem_limit_bytes=48 * 2**20)
    hbm = pl.BlockSpec(memory_space=pltpu.HBM)
    own = [
        pltpu.with_memory_space_constraint(a, pltpu.HBM)
        for a in (index, tile_count, tile_blocks)
    ]
    own_scratch = [
        pltpu.SMEM(index.shape, index.dtype),
        pltpu.SMEM(tile_count.shape, tile_count.dtype),
        pltpu.VMEM(tile_blocks.shape, tile_blocks.dtype),
        pltpu.SemaphoreType.DMA((3,)),
    ]
    own_panels = pl.pallas_call(
        own_kernel,
        out_shape=panels_shape,
        in_specs=[hbm] * 3,
        out_specs=VMEM(),
        scratch_shapes=own_scratch,
        compiler_params=params,
        name="own_tiles",
    )(*own)
    far = list(range(slots // 2, slots))
    near = list(reversed(range(slots // 2)))
    rest = near + far[1:]
    first = far[:1]
    panels, chip_q, *far_messages = pl.pallas_call(
        functools.partial(far_kernel, chips, first),
        out_shape=[panels_shape, q_shape] + [message] * len(first),
        in_specs=[pl.BlockSpec(memory_space=pl.ANY)] * 2 + [VMEM()] * 4,
        out_specs=[VMEM()] * (2 + len(first)),
        scratch_shapes=own_scratch[:2] + [pltpu.SemaphoreType.DMA((2,))],
        input_output_aliases={5: 0},
        compiler_params=params,
        name="pack_far",
    )(other_index, other_count, other_tiles, q_block, other_q, own_panels)
    panels, *rest_messages = pl.pallas_call(
        functools.partial(near_kernel, chips, rest),
        out_shape=[panels_shape] + [message] * len(rest),
        in_specs=[pl.BlockSpec(memory_space=pl.ANY)] * 2 + [VMEM()] * 3,
        out_specs=[VMEM()] * (1 + len(rest)),
        scratch_shapes=own_scratch[:2] + [pltpu.SemaphoreType.DMA((2,))],
        input_output_aliases={3: 0},
        compiler_params=params,
        name="pack_near",
    )(other_index, other_count, other_tiles, panels, chip_q)
    messages = dict(zip(first + rest, far_messages + rest_messages, strict=True))
    received = {
        k: lax.ppermute(messages[k], "row", [
            (d, d ^ (2 * (2 * k + d % 2))) for d in range(devices) if 2 * k + d % 2
        ])
        for k in first + rest
    }

    rows_panels, direct, mirror = pl.pallas_call(
        direct_kernel,
        out_shape=[rows_panels_shape, half_shape, half_shape],
        in_specs=[hbm] * 3 + [VMEM()] * 2,
        out_specs=[VMEM()] * 3,
        scratch_shapes=own_scratch,
        compiler_params=params,
        cost_estimate=pl.CostEstimate(flops=10000000000, bytes_accessed=0, transcendentals=0),
            name="direct_local",
    )(*own, panels, chip_q)

    def gather(kernel, sources, sums, name, outs, passed=()):
        sums = list(sums)
        return pl.pallas_call(
            functools.partial(kernel, sources),
            out_shape=[half_shape] * outs + [message] * len(passed),
            in_specs=[VMEM()] * (1 + len(sums) + len(sources) + len(passed)),
            out_specs=[VMEM()] * (outs + len(passed)),
            input_output_aliases={
                1 + len(sums) + len(sources) + n: outs + n for n in range(len(passed))
            },
            compiler_params=params,
            cost_estimate=pl.CostEstimate(
                flops=10**10, bytes_accessed=0, transcendentals=0
            ),
            name=name,
        )(rows_panels, *sums,
          *((received if mine else other)[k] for k, mine in sources), *passed)

    *late, last = near + far[1:]
    other = {k: swap(received[k]) for k in [far[0], *late, last]}
    direct, mirror = gather(
        gather_kernel, [(far[0], True), (far[0], False)], (direct, mirror),
        "gather_first", 2,
    )
    (base,) = gather(
        join_kernel,
        [(k, mine) for k in late for mine in (True, False)] + [(last, True)],
        (direct, mirror), "gather_most", 1,
    )
    return pl.pallas_call(
        functools.partial(final_kernel, last, 1.0 / math.sqrt(rows * devices)),
        out_shape=half_shape,
        in_specs=[VMEM()] * 3,
        out_specs=hbm,
        scratch_shapes=[pltpu.VMEM((rows, columns), wide), pltpu.SemaphoreType.DMA(())],
        compiler_params=params,
        name="gather_last",
    )(rows_panels, base, other[last])


def solution(mesh):
    return jax.shard_map(
        functools.partial(on_device, mesh.shape["row"]),
        mesh=mesh,
        in_specs=(
            P(("grp", "row"), None, None),
            P(("grp", "row"), None),
            P(("grp", "row"), None),
            P(("grp", "row")),
        ),
        out_specs=P(("grp", "row"), None),
        check_vma=False,
    )
```

```python
import functools
import math

import jax
import jax.numpy as jnp
from jax import lax
from jax.experimental import pallas as pl
from jax.experimental.pallas import tpu as pltpu
from jax.sharding import PartitionSpec as P

TOP = 32700.0
STEPS = 16.0
LEAST = 1e-30


def place():
    me = lax.axis_index("row")
    return me // 2, me % 2


def scale_of(code):
    return jnp.exp2(code * (1.0 / STEPS))


def encode(x):
    top = jnp.maximum(jnp.max(jnp.abs(x), axis=0, keepdims=True), LEAST)
    code = jnp.ceil(jnp.log2(top) * STEPS)
    values = jnp.round(x * (TOP / scale_of(code)))
    return values.astype(jnp.int32).astype(jnp.int16), code


def live_tiles(count):
    live = count[0]
    for r in range(1, count.shape[0]):
        live = live + count[r]
    return live


def put_tiles(index, count, tiles, panels, chip_blocks):
    chip, core = place()
    tile = tiles.shape[1]
    local = panels.shape[0] // chip_blocks - 1

    def put(s, carry):
        i, j = index[0, s], index[1, s]
        cls = chip ^ (j // chip_blocks)

        @pl.when((cls == 0) | (cls % 2 == core))
        def _():
            slot = jnp.where(cls == 0, local, cls // 2)
            panel = slot * chip_blocks + j % chip_blocks
            at = pl.multiple_of((i % (chip_blocks // 2)) * tile, tile)
            panels[panel, pl.ds(at, tile), :] = tiles[s]

        return carry

    lax.fori_loop(0, live_tiles(count), put, 0)


def fetch(sems, *pairs):
    copies = [
        pltpu.make_async_copy(a, b, sems.at[n]) for n, (a, b) in enumerate(pairs)
    ]
    for copy in copies:
        copy.start()
    return copies


def own_kernel(index_ref, count_ref, tiles_ref, panels, index, count, tiles, sems):
    copies = fetch(sems, (index_ref, index), (count_ref, count), (tiles_ref, tiles))
    panels[...] = jnp.zeros_like(panels)
    for copy in copies:
        copy.wait()
    put_tiles(index, count, tiles, panels, 2 * panels.shape[1] // panels.shape[2])


def direct_kernel(
    index_ref, count_ref, tiles_ref, chip_q, rows_panels, direct,
    index, count, tiles, sems,
):
    copies = fetch(sems, (index_ref, index), (count_ref, count), (tiles_ref, tiles))
    rows_panels[...] = jnp.zeros_like(rows_panels)
    for copy in copies:
        copy.wait()
    tile = tiles.shape[1]
    rows = rows_panels.shape[1]
    chip_blocks = 2 * rows // tile
    chip, _ = place()

    def put(s, carry):
        i, j = index[0, s], index[1, s]
        panel = (chip ^ (j // chip_blocks)) * chip_blocks + j % chip_blocks
        at = pl.multiple_of((i % (rows // tile)) * tile, tile)
        rows_panels[panel, pl.ds(at, tile), :] = tiles[s]
        return carry

    lax.fori_loop(0, live_tiles(count), put, 0)
    direct[...] = direct_sum(rows_panels, 0, split(chip_q[...], tile))


def write_message(message, blocks):
    tile = message.shape[1]
    codes = []
    for b, x in enumerate(blocks):
        values, code = encode(x)
        message[b * tile:(b + 1) * tile, :] = values
        codes.append(code)
    which = lax.broadcasted_iota(jnp.int32, (16, tile), 0)
    tail = jnp.zeros((16, tile), jnp.float32)
    for b, code in enumerate(codes):
        tail = jnp.where(which == b, code, tail)
    message[len(blocks) * tile:, :] = tail.astype(jnp.int32).astype(jnp.int16)


def read_message(message):
    tile = message.shape[1]
    blocks = message.shape[0] // tile
    tail = message[blocks * tile:, :].astype(jnp.int32).astype(jnp.float32)
    scales = scale_of(tail) * (1.0 / TOP)
    return [
        message[b * tile:(b + 1) * tile, :].astype(jnp.int32).astype(jnp.float32)
        * scales[b:b + 1, :]
        for b in range(blocks)
    ]


def mirrored_blocks(parts, blocks):
    tile = parts[0][1].shape[2]
    sums = []
    for b in range(0, blocks, 2):
        pair = sum(
            jnp.dot(
                q_t,
                jnp.concatenate([panels[g + b], panels[g + b + 1]], axis=1),
                preferred_element_type=jnp.float32,
            )
            for q_t, panels, g in parts
        )
        sums += [pair[:, :tile], pair[:, tile:]]
    return sums


def direct_sum(panels, start, blocks):
    total = None
    for b in range(0, len(blocks), 2):
        pair = jnp.concatenate([panels[start + b], panels[start + b + 1]], axis=1)
        q = jnp.concatenate(blocks[b:b + 2], axis=0).astype(jnp.bfloat16)
        part = jnp.dot(pair, q, preferred_element_type=jnp.float32)
        total = part if total is None else total + part
    return total


def split(x, tile):
    return [x[at:at + tile, :] for at in range(0, x.shape[0], tile)]


def in_lower_half(chips):
    return place()[0] < chips // 2


def far_kernel(
    chips, k, index_ref, count_ref, tiles, own_q, other_q, own_panels,
    chip_q, message, panels, index, count, sems,
):
    rows, tile = own_q.shape[0], tiles.shape[1]
    chip_blocks = 2 * rows // tile
    _, core = place()
    chip_q[pl.ds(pl.multiple_of(core * rows, rows), rows), :] = own_q[...]
    chip_q[pl.ds(pl.multiple_of((1 - core) * rows, rows), rows), :] = other_q[...]

    @pl.when(in_lower_half(chips))
    def _():
        copies = fetch(sems, (index_ref, index), (count_ref, count))
        panels[...] = jnp.zeros_like(panels)
        own_t, other_t = own_q[...].T, other_q[...].T
        for copy in copies:
            copy.wait()
        put_tiles(index, count, tiles, panels, chip_blocks)
        first = k * chip_blocks
        parts = [(own_t, own_panels, first), (other_t, panels, first)]
        write_message(message, mirrored_blocks(parts, chip_blocks))

    @pl.when(jnp.logical_not(in_lower_half(chips)))
    def _():
        write_message(message, split(chip_q[...].astype(jnp.float32), tile))


def near_kernel(
    chips, slots, index_ref, count_ref, tiles, own_panels, far_panels, chip_q, *refs
):
    *messages, mirror, panels, index, count, sems = refs
    rows, tile = own_panels.shape[1:]
    chip_blocks = 2 * rows // tile
    chip, core = place()

    def write(other_panels):
        def transposed(at):
            return chip_q[pl.ds(pl.multiple_of(at * rows, rows), rows), :].T

        own_t, other_t = transposed(core), transposed(1 - core)

        def mirrored(first, blocks):
            return mirrored_blocks(
                [(own_t, own_panels, first), (other_t, other_panels, first)], blocks
            )

        q = split(chip_q[...].astype(jnp.float32), tile)
        for k, message in zip(slots, messages, strict=True):
            up = chip < (chip ^ (2 * k + core))
            blocks = mirrored(k * chip_blocks, chip_blocks)
            write_message(
                message, [jnp.where(up, m, x) for m, x in zip(blocks, q, strict=True)]
            )
        half = chip_blocks // 2
        local = mirrored(other_panels.shape[0] - chip_blocks + core * half, half)
        for b, m in enumerate(local):
            mirror[b * tile:(b + 1) * tile, :] = m

    @pl.when(in_lower_half(chips))
    def _():
        write(far_panels)

    @pl.when(jnp.logical_not(in_lower_half(chips)))
    def _():
        copies = fetch(sems, (index_ref, index), (count_ref, count))
        panels[...] = jnp.zeros_like(panels)
        for copy in copies:
            copy.wait()
        put_tiles(index, count, tiles, panels, chip_blocks)
        write(panels)


def is_low(k, mine):
    chip, core = place()
    cls = 2 * k + (core if mine else 1 - core)
    return (chip ^ cls) < chip, cls


def own_half(blocks):
    _, core = place()
    half = len(blocks) // 2
    return [
        jnp.where(core == 0, a, b)
        for a, b in zip(blocks[:half], blocks[half:], strict=True)
    ]


def gather_part(sources, rows_panels, direct, mirror, messages):
    total = direct[...]
    mirrored = split(mirror[...], rows_panels.shape[2])
    for (k, mine), message in zip(sources, messages, strict=True):
        low, cls = is_low(k, mine)
        blocks = read_message(message)
        total = total + direct_sum(rows_panels, cls * len(blocks), blocks)
        mirrored = [
            m + jnp.where(low, x, 0.0)
            for m, x in zip(mirrored, own_half(blocks), strict=True)
        ]
    return total, mirrored


def gather_kernel(sources, rows_panels, direct, mirror, *refs):
    *messages, direct_out, mirror_out = refs
    tile = rows_panels.shape[2]
    total, mirrored = gather_part(sources, rows_panels, direct, mirror, messages)
    direct_out[...] = total
    for b, m in enumerate(mirrored):
        mirror_out[b * tile:(b + 1) * tile, :] = m


def join_kernel(sources, rows_panels, direct, mirror, *refs):
    *messages, base = refs
    tile = rows_panels.shape[2]
    total, mirrored = gather_part(sources, rows_panels, direct, mirror, messages)
    for b, (block, m) in enumerate(zip(split(total, tile), mirrored, strict=True)):
        base[b * tile:(b + 1) * tile, :] = block + m.T


def final_kernel(k, factor, rows_panels, base, message, out, result, sem):
    tile = rows_panels.shape[2]
    low, cls = is_low(k, False)

    @pl.when(low)
    def _():
        for b, x in enumerate(own_half(read_message(message))):
            at = slice(b * tile, (b + 1) * tile)
            result[at, :] = (base[at, :] + x.T) * factor

    @pl.when(jnp.logical_not(low))
    def _():
        blocks = read_message(message)
        total = direct_sum(rows_panels, cls * len(blocks), blocks)
        result[...] = (base[...] + total) * factor

    copy = pltpu.make_async_copy(result, out, sem)
    copy.start()
    copy.wait()


VMEM = functools.partial(pl.BlockSpec, memory_space=pltpu.VMEM)
SMEM = functools.partial(pl.BlockSpec, memory_space=pltpu.SMEM)


def on_device(devices, tile_blocks, q_block, tile_index, tile_count):
    tile = tile_blocks.shape[1]
    rows, columns = q_block.shape
    chips = devices // 2
    slots = chips // 2
    chip_rows = 2 * rows
    chip_blocks = chip_rows // tile
    wide = jnp.float32
    other_core = [(d, d ^ 1) for d in range(devices)]

    def swap(x):
        return lax.ppermute(x, "row", other_core)

    index = tile_index.T
    other_tiles = swap(tile_blocks)
    other_q = swap(q_block)
    other_index = swap(index)
    other_count = swap(tile_count)

    panels_shape = jax.ShapeDtypeStruct(
        ((slots + 1) * chip_blocks, rows, tile), jnp.bfloat16
    )
    rows_panels_shape = jax.ShapeDtypeStruct(
        (chips * chip_blocks, rows, tile), jnp.bfloat16
    )
    q_shape = jax.ShapeDtypeStruct((chip_rows, columns), jnp.bfloat16)
    message = jax.ShapeDtypeStruct((chip_rows + 16, columns), jnp.int16)
    half_shape = jax.ShapeDtypeStruct((rows, columns), wide)
    params = pltpu.CompilerParams(vmem_limit_bytes=48 * 2**20)
    hbm = pl.BlockSpec(memory_space=pltpu.HBM)
    own = [
        pltpu.with_memory_space_constraint(a, pltpu.HBM)
        for a in (index, tile_count, tile_blocks)
    ]
    own_scratch = [
        pltpu.SMEM(index.shape, index.dtype),
        pltpu.SMEM(tile_count.shape, tile_count.dtype),
        pltpu.VMEM(tile_blocks.shape, tile_blocks.dtype),
        pltpu.SemaphoreType.DMA((3,)),
    ]
    own_panels = pl.pallas_call(
        own_kernel,
        out_shape=panels_shape,
        in_specs=[hbm] * 3,
        out_specs=VMEM(),
        scratch_shapes=own_scratch,
        compiler_params=params,
        name="own_tiles",
    )(*own)
    far = list(range(slots // 2, slots))
    near = list(reversed(range(slots // 2)))
    rest = near + far[1:]
    other = (other_index, other_count, other_tiles)
    other_specs = [pl.BlockSpec(memory_space=pl.ANY)] * 2 + [VMEM()]
    other_scratch = [*own_scratch[:2], pltpu.SemaphoreType.DMA((2,))]
    chip_q, far_message, far_panels = pl.pallas_call(
        functools.partial(far_kernel, chips, far[0]),
        out_shape=[q_shape, message, panels_shape],
        in_specs=other_specs + [VMEM()] * 3,
        out_specs=[VMEM()] * 3,
        scratch_shapes=other_scratch,
        compiler_params=params,
        name="pack_far",
    )(*other, q_block, other_q, own_panels)
    *rest_messages, mirror = pl.pallas_call(
        functools.partial(near_kernel, chips, rest),
        out_shape=[message] * len(rest) + [half_shape],
        in_specs=other_specs + [VMEM()] * 3,
        out_specs=[VMEM()] * (len(rest) + 1),
        scratch_shapes=[pltpu.VMEM(panels_shape.shape, jnp.bfloat16), *other_scratch],
        compiler_params=params,
        name="pack_near",
    )(*other, own_panels, far_panels, chip_q)
    messages = dict(zip(far[:1] + rest, [far_message, *rest_messages], strict=True))
    received = {
        k: lax.ppermute(messages[k], "row", [
            (d, d ^ (2 * (2 * k + d % 2))) for d in range(devices) if 2 * k + d % 2
        ])
        for k in far[:1] + rest
    }

    rows_panels, direct = pl.pallas_call(
        direct_kernel,
        out_shape=[rows_panels_shape, half_shape],
        in_specs=[hbm] * 3 + [VMEM()],
        out_specs=[VMEM()] * 2,
        scratch_shapes=own_scratch,
        compiler_params=params,
        cost_estimate=pl.CostEstimate(
            flops=10**10, bytes_accessed=0, transcendentals=0
        ),
        name="direct_local",
    )(*own, chip_q)

    def gather(kernel, sources, sums, name, outs, passed=()):
        sums = list(sums)
        return pl.pallas_call(
            functools.partial(kernel, sources),
            out_shape=[half_shape] * outs + [message] * len(passed),
            in_specs=[VMEM()] * (1 + len(sums) + len(sources) + len(passed)),
            out_specs=[VMEM()] * (outs + len(passed)),
            input_output_aliases={
                1 + len(sums) + len(sources) + n: outs + n for n in range(len(passed))
            },
            compiler_params=params,
            cost_estimate=pl.CostEstimate(
                flops=10**10, bytes_accessed=0, transcendentals=0
            ),
            name=name,
        )(rows_panels, *sums,
          *((received if mine else other)[k] for k, mine in sources), *passed)

    *late, last = near + far[1:]
    other = {k: swap(received[k]) for k in [far[0], *late, last]}
    direct, mirror = gather(
        gather_kernel, [(far[0], True), (far[0], False)], (direct, mirror),
        "gather_first", 2,
    )
    (base,) = gather(
        join_kernel,
        [(k, mine) for k in late for mine in (True, False)] + [(last, True)],
        (direct, mirror), "gather_most", 1,
    )
    return pl.pallas_call(
        functools.partial(final_kernel, last, 1.0 / math.sqrt(rows * devices)),
        out_shape=half_shape,
        in_specs=[VMEM()] * 3,
        out_specs=hbm,
        scratch_shapes=[pltpu.VMEM((rows, columns), wide), pltpu.SemaphoreType.DMA(())],
        compiler_params=params,
        name="gather_last",
    )(rows_panels, base, other[last])


def solution(mesh):
    return jax.shard_map(
        functools.partial(on_device, mesh.shape["row"]),
        mesh=mesh,
        in_specs=(
            P(("grp", "row"), None, None),
            P(("grp", "row"), None),
            P(("grp", "row"), None),
            P(("grp", "row")),
        ),
        out_specs=P(("grp", "row"), None),
        check_vma=False,
    )
```

```python
import functools
import math

import jax
import jax.numpy as jnp
from jax import lax
from jax.experimental import pallas as pl
from jax.experimental.pallas import tpu as pltpu
from jax.sharding import PartitionSpec as P

TOP = 32700.0
STEPS = 16.0
LEAST = 1e-30


def place():
    me = lax.axis_index("row")
    return me // 2, me % 2


def scale_of(code):
    return jnp.exp2(code * (1.0 / STEPS))


def encode(x):
    top = jnp.maximum(jnp.max(jnp.abs(x), axis=0, keepdims=True), LEAST)
    code = jnp.ceil(jnp.log2(top) * STEPS)
    values = jnp.round(x * (TOP / scale_of(code)))
    return values.astype(jnp.int32).astype(jnp.int16), code


def live_tiles(count):
    live = count[0]
    for r in range(1, count.shape[0]):
        live = live + count[r]
    return live


def put_tiles(index, count, tiles, panels, chip_blocks):
    chip, core = place()
    tile = tiles.shape[1]
    spare = panels.shape[0] - 1
    local = spare // chip_blocks - 1
    step = 2 if tiles.shape[0] % 2 == 0 else 1
    live = live_tiles(count)

    def put(n, carry):
        for s in [n * step + e for e in range(step)]:
            i, j = index[0, s], index[1, s]
            cls = chip ^ (j // chip_blocks)
            slot = jnp.where(cls == 0, local, cls // 2)
            wanted = (s < live) & ((cls == 0) | (cls % 2 == core))
            panel = jnp.where(wanted, slot * chip_blocks + j % chip_blocks, spare)
            at = pl.multiple_of((i % (chip_blocks // 2)) * tile, tile)
            panels[panel, pl.ds(at, tile), :] = tiles[s]
        return carry

    lax.fori_loop(0, (live + step - 1) // step, put, 0)


def fetch(sems, *pairs):
    copies = [
        pltpu.make_async_copy(a, b, sems.at[n]) for n, (a, b) in enumerate(pairs)
    ]
    for copy in copies:
        copy.start()
    return copies


def own_kernel(index_ref, count_ref, tiles_ref, panels, index, count, tiles, sems):
    copies = fetch(sems, (index_ref, index), (count_ref, count), (tiles_ref, tiles))
    panels[...] = jnp.zeros_like(panels)
    for copy in copies:
        copy.wait()
    put_tiles(index, count, tiles, panels, 2 * panels.shape[1] // panels.shape[2])


def direct_kernel(
    index_ref, count_ref, tiles_ref, chip_q, rows_panels, direct,
    index, count, tiles, sems,
):
    copies = fetch(sems, (index_ref, index), (count_ref, count), (tiles_ref, tiles))
    rows_panels[...] = jnp.zeros_like(rows_panels)
    for copy in copies:
        copy.wait()
    tile = tiles.shape[1]
    rows = rows_panels.shape[1]
    chip_blocks = 2 * rows // tile
    chip, _ = place()

    def put(s, carry):
        i, j = index[0, s], index[1, s]
        panel = (chip ^ (j // chip_blocks)) * chip_blocks + j % chip_blocks
        at = pl.multiple_of((i % (rows // tile)) * tile, tile)
        rows_panels[panel, pl.ds(at, tile), :] = tiles[s]
        return carry

    lax.fori_loop(0, live_tiles(count), put, 0)
    direct[...] = direct_sum(rows_panels, 0, split(chip_q[...], tile))


def write_message(message, blocks):
    tile = message.shape[1]
    codes = []
    for b, x in enumerate(blocks):
        values, code = encode(x)
        message[b * tile:(b + 1) * tile, :] = values
        codes.append(code)
    which = lax.broadcasted_iota(jnp.int32, (16, tile), 0)
    tail = jnp.zeros((16, tile), jnp.float32)
    for b, code in enumerate(codes):
        tail = jnp.where(which == b, code, tail)
    message[len(blocks) * tile:, :] = tail.astype(jnp.int32).astype(jnp.int16)


def read_message(message):
    tile = message.shape[1]
    blocks = message.shape[0] // tile
    tail = message[blocks * tile:, :].astype(jnp.int32).astype(jnp.float32)
    scales = scale_of(tail) * (1.0 / TOP)
    return [
        message[b * tile:(b + 1) * tile, :].astype(jnp.int32).astype(jnp.float32)
        * scales[b:b + 1, :]
        for b in range(blocks)
    ]


def mirrored_blocks(parts, blocks):
    tile = parts[0][1].shape[2]
    sums = []
    for b in range(0, blocks, 2):
        pair = sum(
            jnp.dot(
                q_t,
                jnp.concatenate([panels[g + b], panels[g + b + 1]], axis=1),
                preferred_element_type=jnp.float32,
            )
            for q_t, panels, g in parts
        )
        sums += [pair[:, :tile], pair[:, tile:]]
    return sums


def direct_sum(panels, start, blocks):
    total = None
    for b in range(0, len(blocks), 2):
        pair = jnp.concatenate([panels[start + b], panels[start + b + 1]], axis=1)
        q = jnp.concatenate(blocks[b:b + 2], axis=0).astype(jnp.bfloat16)
        part = jnp.dot(pair, q, preferred_element_type=jnp.float32)
        total = part if total is None else total + part
    return total


def split(x, tile):
    return [x[at:at + tile, :] for at in range(0, x.shape[0], tile)]


def in_lower_half(chips):
    return place()[0] < chips // 2


def far_kernel(
    chips, k, index_ref, count_ref, tiles, own_q, other_q, own_panels,
    chip_q, message, panels, sums, index, count, sems,
):
    rows, tile = own_q.shape[0], tiles.shape[1]
    chip_blocks = 2 * rows // tile
    _, core = place()
    chip_q[pl.ds(pl.multiple_of(core * rows, rows), rows), :] = own_q[...]
    chip_q[pl.ds(pl.multiple_of((1 - core) * rows, rows), rows), :] = other_q[...]

    @pl.when(in_lower_half(chips))
    def _():
        copies = fetch(sems, (index_ref, index), (count_ref, count))
        panels[...] = jnp.zeros_like(panels)
        first = class_of(k, core, True, chips) // 2 * chip_blocks
        mine = mirrored_blocks([(own_q[...].T, own_panels, first)], chip_blocks)
        for b, m in enumerate(mine):
            sums[b] = m
        other_t = other_q[...].T
        for copy in copies:
            copy.wait()
        put_tiles(index, count, tiles, panels, chip_blocks)
        theirs = mirrored_blocks([(other_t, panels, first)], chip_blocks)
        write_message(message, [sums[b] + m for b, m in enumerate(theirs)])

    @pl.when(jnp.logical_not(in_lower_half(chips)))
    def _():
        write_message(message, split(chip_q[...].astype(jnp.float32), tile))


def near_kernel(
    chips, slots, index_ref, count_ref, tiles, own_panels, far_panels, chip_q, *refs
):
    *messages, mirror, panels, index, count, sems = refs
    rows, tile = own_panels.shape[1:]
    chip_blocks = 2 * rows // tile
    chip, core = place()

    def write(other_panels):
        def transposed(at):
            return chip_q[pl.ds(pl.multiple_of(at * rows, rows), rows), :].T

        own_t, other_t = transposed(core), transposed(1 - core)

        def mirrored(first, blocks):
            return mirrored_blocks(
                [(own_t, own_panels, first), (other_t, other_panels, first)], blocks
            )

        q = split(chip_q[...].astype(jnp.float32), tile)
        for k, message in zip(slots, messages, strict=True):
            cls = class_of(k, core, in_lower_half(chips), chips)
            up = chip < (chip ^ cls)
            blocks = mirrored(cls // 2 * chip_blocks, chip_blocks)
            write_message(
                message, [jnp.where(up, m, x) for m, x in zip(blocks, q, strict=True)]
            )
        half = chip_blocks // 2
        last = other_panels.shape[0] - 1 - chip_blocks
        local = mirrored(last + core * half, half)
        for b, m in enumerate(local):
            mirror[b * tile:(b + 1) * tile, :] = m

    @pl.when(in_lower_half(chips))
    def _():
        write(far_panels)

    @pl.when(jnp.logical_not(in_lower_half(chips)))
    def _():
        copies = fetch(sems, (index_ref, index), (count_ref, count))
        panels[...] = jnp.zeros_like(panels)
        for copy in copies:
            copy.wait()
        put_tiles(index, count, tiles, panels, chip_blocks)
        write(panels)


def class_of(k, core, from_lower, chips):
    if k < chips // 4:
        return 2 * k + core
    other = chips // 2 + chips // 4 - 1 - k
    if isinstance(core, int):
        return 2 * (other if core and from_lower else k) + core
    return 2 * jnp.where((core == 1) & from_lower, other, k) + core


def is_low(chips, k, mine):
    chip, core = place()
    carrier = core if mine else 1 - core
    cls = class_of(k, carrier, jnp.logical_not(in_lower_half(chips)), chips)
    return (chip ^ cls) < chip, cls


def own_half(blocks):
    _, core = place()
    half = len(blocks) // 2
    return [
        jnp.where(core == 0, a, b)
        for a, b in zip(blocks[:half], blocks[half:], strict=True)
    ]


def gather_part(chips, sources, rows_panels, direct, mirror, messages):
    total = direct[...]
    mirrored = split(mirror[...], rows_panels.shape[2])
    for (k, mine), message in zip(sources, messages, strict=True):
        low, cls = is_low(chips, k, mine)
        blocks = read_message(message)
        total = total + direct_sum(rows_panels, cls * len(blocks), blocks)
        mirrored = [
            m + jnp.where(low, x, 0.0)
            for m, x in zip(mirrored, own_half(blocks), strict=True)
        ]
    return total, mirrored


def gather_kernel(chips, sources, rows_panels, direct, mirror, *refs):
    *messages, direct_out, mirror_out = refs
    tile = rows_panels.shape[2]
    total, mirrored = gather_part(chips, sources, rows_panels, direct, mirror, messages)
    direct_out[...] = total
    for b, m in enumerate(mirrored):
        mirror_out[b * tile:(b + 1) * tile, :] = m


def join_kernel(chips, sources, rows_panels, direct, mirror, *refs):
    *messages, base = refs
    tile = rows_panels.shape[2]
    total, mirrored = gather_part(chips, sources, rows_panels, direct, mirror, messages)
    for b, (block, m) in enumerate(zip(split(total, tile), mirrored, strict=True)):
        base[b * tile:(b + 1) * tile, :] = block + m.T


def final_kernel(chips, k, factor, rows_panels, base, message, out, result, sem):
    tile = rows_panels.shape[2]
    low, cls = is_low(chips, k, False)

    @pl.when(low)
    def _():
        for b, x in enumerate(own_half(read_message(message))):
            at = slice(b * tile, (b + 1) * tile)
            result[at, :] = (base[at, :] + x.T) * factor

    @pl.when(jnp.logical_not(low))
    def _():
        blocks = read_message(message)
        total = direct_sum(rows_panels, cls * len(blocks), blocks)
        result[...] = (base[...] + total) * factor

    copy = pltpu.make_async_copy(result, out, sem)
    copy.start()
    copy.wait()


VMEM = functools.partial(pl.BlockSpec, memory_space=pltpu.VMEM)
SMEM = functools.partial(pl.BlockSpec, memory_space=pltpu.SMEM)


def on_device(devices, tile_blocks, q_block, tile_index, tile_count):
    tile = tile_blocks.shape[1]
    rows, columns = q_block.shape
    chips = devices // 2
    slots = chips // 2
    chip_rows = 2 * rows
    chip_blocks = chip_rows // tile
    wide = jnp.float32
    other_core = [(d, d ^ 1) for d in range(devices)]

    def swap(x):
        return lax.ppermute(x, "row", other_core)

    index = tile_index.T
    other_tiles = swap(tile_blocks)
    other_q = swap(q_block)
    other_index = swap(index)
    other_count = swap(tile_count)

    panels_shape = jax.ShapeDtypeStruct(
        ((slots + 1) * chip_blocks + 1, rows, tile), jnp.bfloat16
    )
    rows_panels_shape = jax.ShapeDtypeStruct(
        (chips * chip_blocks, rows, tile), jnp.bfloat16
    )
    q_shape = jax.ShapeDtypeStruct((chip_rows, columns), jnp.bfloat16)
    message = jax.ShapeDtypeStruct((chip_rows + 16, columns), jnp.int16)
    half_shape = jax.ShapeDtypeStruct((rows, columns), wide)
    params = pltpu.CompilerParams(vmem_limit_bytes=48 * 2**20)
    hbm = pl.BlockSpec(memory_space=pltpu.HBM)
    own = [
        pltpu.with_memory_space_constraint(a, pltpu.HBM)
        for a in (index, tile_count, tile_blocks)
    ]
    own_scratch = [
        pltpu.SMEM(index.shape, index.dtype),
        pltpu.SMEM(tile_count.shape, tile_count.dtype),
        pltpu.VMEM(tile_blocks.shape, tile_blocks.dtype),
        pltpu.SemaphoreType.DMA((3,)),
    ]
    own_panels = pl.pallas_call(
        own_kernel,
        out_shape=panels_shape,
        in_specs=[hbm] * 3,
        out_specs=VMEM(),
        scratch_shapes=own_scratch,
        compiler_params=params,
        name="own_tiles",
    )(*own)
    far = list(range(slots // 2, slots))
    near = list(reversed(range(slots // 2)))
    rest = near + far[1:]
    other = (other_index, other_count, other_tiles)
    other_specs = [pl.BlockSpec(memory_space=pl.ANY)] * 2 + [VMEM()]
    other_scratch = [*own_scratch[:2], pltpu.SemaphoreType.DMA((2,))]
    chip_q, far_message, far_panels = pl.pallas_call(
        functools.partial(far_kernel, chips, far[0]),
        out_shape=[q_shape, message, panels_shape],
        in_specs=other_specs + [VMEM()] * 3,
        out_specs=[VMEM()] * 3,
        scratch_shapes=[pltpu.VMEM((chip_blocks, tile, columns), wide), *other_scratch],
        compiler_params=params,
        name="pack_far",
    )(*other, q_block, other_q, own_panels)
    *rest_messages, mirror = pl.pallas_call(
        functools.partial(near_kernel, chips, rest),
        out_shape=[message] * len(rest) + [half_shape],
        in_specs=other_specs + [VMEM()] * 3,
        out_specs=[VMEM()] * (len(rest) + 1),
        scratch_shapes=[pltpu.VMEM(panels_shape.shape, jnp.bfloat16), *other_scratch],
        compiler_params=params,
        name="pack_near",
    )(*other, own_panels, far_panels, chip_q)
    messages = dict(zip(far[:1] + rest, [far_message, *rest_messages], strict=True))
    received = {
        k: lax.ppermute(messages[k], "row", [
            (d, d ^ (2 * cls))
            for d in range(devices)
            if (cls := class_of(k, d % 2, d < devices // 2, chips))
        ])
        for k in far[:1] + rest
    }

    rows_panels, direct = pl.pallas_call(
        direct_kernel,
        out_shape=[rows_panels_shape, half_shape],
        in_specs=[hbm] * 3 + [VMEM()],
        out_specs=[VMEM()] * 2,
        scratch_shapes=own_scratch,
        compiler_params=params,
        cost_estimate=pl.CostEstimate(
            flops=10**10, bytes_accessed=0, transcendentals=0
        ),
        name="direct_local",
    )(*own, chip_q)

    def gather(kernel, sources, sums, name, outs, passed=()):
        sums = list(sums)
        return pl.pallas_call(
            functools.partial(kernel, chips, sources),
            out_shape=[half_shape] * outs + [message] * len(passed),
            in_specs=[VMEM()] * (1 + len(sums) + len(sources) + len(passed)),
            out_specs=[VMEM()] * (outs + len(passed)),
            input_output_aliases={
                1 + len(sums) + len(sources) + n: outs + n for n in range(len(passed))
            },
            compiler_params=params,
            cost_estimate=pl.CostEstimate(
                flops=10**10, bytes_accessed=0, transcendentals=0
            ),
            name=name,
        )(rows_panels, *sums,
          *((received if mine else other)[k] for k, mine in sources), *passed)

    *late, last = near + far[1:]
    other = {k: swap(received[k]) for k in [far[0], *late, last]}
    direct, mirror = gather(
        gather_kernel, [(far[0], True), (far[0], False)], (direct, mirror),
        "gather_first", 2,
    )
    (base,) = gather(
        join_kernel,
        [(k, mine) for k in late for mine in (True, False)] + [(last, True)],
        (direct, mirror), "gather_most", 1,
    )
    return pl.pallas_call(
        functools.partial(final_kernel, chips, last, 1.0 / math.sqrt(rows * devices)),
        out_shape=half_shape,
        in_specs=[VMEM()] * 3,
        out_specs=hbm,
        scratch_shapes=[pltpu.VMEM((rows, columns), wide), pltpu.SemaphoreType.DMA(())],
        compiler_params=params,
        name="gather_last",
    )(rows_panels, base, other[last])


def solution(mesh):
    return jax.shard_map(
        functools.partial(on_device, mesh.shape["row"]),
        mesh=mesh,
        in_specs=(
            P(("grp", "row"), None, None),
            P(("grp", "row"), None),
            P(("grp", "row"), None),
            P(("grp", "row")),
        ),
        out_specs=P(("grp", "row"), None),
        check_vma=False,
    )
```

```python
import functools
import math

import jax
import jax.numpy as jnp
from jax import lax
from jax.experimental import pallas as pl
from jax.experimental.pallas import tpu as pltpu
from jax.sharding import PartitionSpec as P

TOP = 32700.0
STEPS = 16.0
LEAST = 1e-30


def place():
    me = lax.axis_index("row")
    return me // 2, me % 2


def scale_of(code):
    return jnp.exp2(code * (1.0 / STEPS))


def encode(x):
    top = jnp.maximum(jnp.max(jnp.abs(x), axis=0, keepdims=True), LEAST)
    code = jnp.ceil(jnp.log2(top) * STEPS)
    values = jnp.round(x * (TOP / scale_of(code)))
    return values.astype(jnp.int32).astype(jnp.int16), code


def live_tiles(count):
    live = count[0]
    for r in range(1, count.shape[0]):
        live = live + count[r]
    return live


def put_tiles(index, count, tiles, panels, chip_blocks):
    chip, core = place()
    tile = tiles.shape[1]
    spare = panels.shape[0] - 1
    local = spare // chip_blocks - 1
    step = 2 if tiles.shape[0] % 2 == 0 else 1
    live = live_tiles(count)

    def put(n, carry):
        for s in [n * step + e for e in range(step)]:
            i, j = index[0, s], index[1, s]
            cls = chip ^ (j // chip_blocks)
            slot = jnp.where(cls == 0, local, cls // 2)
            wanted = (s < live) & ((cls == 0) | (cls % 2 == core))
            panel = jnp.where(wanted, slot * chip_blocks + j % chip_blocks, spare)
            at = pl.multiple_of((i % (chip_blocks // 2)) * tile, tile)
            panels[panel, pl.ds(at, tile), :] = tiles[s]
        return carry

    lax.fori_loop(0, (live + step - 1) // step, put, 0)


def fetch(sems, *pairs):
    copies = [
        pltpu.make_async_copy(a, b, sems.at[n]) for n, (a, b) in enumerate(pairs)
    ]
    for copy in copies:
        copy.start()
    return copies


def own_kernel(index_ref, count_ref, tiles_ref, panels, index, count, tiles, sems):
    copies = fetch(sems, (index_ref, index), (count_ref, count), (tiles_ref, tiles))
    panels[...] = jnp.zeros_like(panels)
    for copy in copies:
        copy.wait()
    put_tiles(index, count, tiles, panels, 2 * panels.shape[1] // panels.shape[2])


def direct_kernel(
    index_ref, count_ref, tiles_ref, chip_q, rows_panels, direct,
    index, count, tiles, sems,
):
    copies = fetch(sems, (index_ref, index), (count_ref, count), (tiles_ref, tiles))
    rows_panels[...] = jnp.zeros_like(rows_panels)
    for copy in copies:
        copy.wait()
    tile = tiles.shape[1]
    rows = rows_panels.shape[1]
    chip_blocks = 2 * rows // tile
    chip, _ = place()

    def put(s, carry):
        i, j = index[0, s], index[1, s]
        panel = (chip ^ (j // chip_blocks)) * chip_blocks + j % chip_blocks
        at = pl.multiple_of((i % (rows // tile)) * tile, tile)
        rows_panels[panel, pl.ds(at, tile), :] = tiles[s]
        return carry

    lax.fori_loop(0, live_tiles(count), put, 0)
    direct[...] = direct_sum(rows_panels, 0, split(chip_q[...], tile))


def write_message(message, blocks):
    tile = message.shape[1]
    codes = []
    for b, x in enumerate(blocks):
        values, code = encode(x)
        message[b * tile:(b + 1) * tile, :] = values
        codes.append(code)
    which = lax.broadcasted_iota(jnp.int32, (16, tile), 0)
    tail = jnp.zeros((16, tile), jnp.float32)
    for b, code in enumerate(codes):
        tail = jnp.where(which == b, code, tail)
    message[len(blocks) * tile:, :] = tail.astype(jnp.int32).astype(jnp.int16)


def read_message(message):
    tile = message.shape[1]
    blocks = message.shape[0] // tile
    tail = message[blocks * tile:, :].astype(jnp.int32).astype(jnp.float32)
    scales = scale_of(tail) * (1.0 / TOP)
    return [
        message[b * tile:(b + 1) * tile, :].astype(jnp.int32).astype(jnp.float32)
        * scales[b:b + 1, :]
        for b in range(blocks)
    ]


def mirrored_blocks(parts, blocks):
    tile = parts[0][1].shape[2]
    sums = []
    for b in range(0, blocks, 2):
        pair = sum(
            jnp.dot(
                q_t,
                jnp.concatenate([panels[g + b], panels[g + b + 1]], axis=1),
                preferred_element_type=jnp.float32,
            )
            for q_t, panels, g in parts
        )
        sums += [pair[:, :tile], pair[:, tile:]]
    return sums


def direct_sum(panels, start, blocks):
    total = None
    for b in range(0, len(blocks), 2):
        pair = jnp.concatenate([panels[start + b], panels[start + b + 1]], axis=1)
        q = jnp.concatenate(blocks[b:b + 2], axis=0).astype(jnp.bfloat16)
        part = jnp.dot(pair, q, preferred_element_type=jnp.float32)
        total = part if total is None else total + part
    return total


def split(x, tile):
    return [x[at:at + tile, :] for at in range(0, x.shape[0], tile)]


def in_lower_half(chips):
    return place()[0] < chips // 2


def far_kernel(
    chips, k, index_ref, count_ref, tiles, own_q, other_q, own_panels,
    chip_q, message, panels, sums, index, count, sems,
):
    rows, tile = own_q.shape[0], tiles.shape[1]
    chip_blocks = 2 * rows // tile
    chip, core = place()
    chip_q[pl.ds(pl.multiple_of(core * rows, rows), rows), :] = own_q[...]
    chip_q[pl.ds(pl.multiple_of((1 - core) * rows, rows), rows), :] = other_q[...]

    @pl.when(in_lower_half(chips))
    def _():
        copies = fetch(sems, (index_ref, index), (count_ref, count))
        panels[...] = jnp.zeros_like(panels)
        first = class_of(k, core, True, chip % 2, chips) // 2 * chip_blocks
        mine = mirrored_blocks([(own_q[...].T, own_panels, first)], chip_blocks)
        for b, m in enumerate(mine):
            sums[b] = m
        other_t = other_q[...].T
        for copy in copies:
            copy.wait()
        put_tiles(index, count, tiles, panels, chip_blocks)
        theirs = mirrored_blocks([(other_t, panels, first)], chip_blocks)
        write_message(message, [sums[b] + m for b, m in enumerate(theirs)])

    @pl.when(jnp.logical_not(in_lower_half(chips)))
    def _():
        write_message(message, split(chip_q[...].astype(jnp.float32), tile))


def near_kernel(
    chips, slots, index_ref, count_ref, tiles, own_panels, far_panels, chip_q, *refs
):
    *messages, mirror, panels, index, count, sems = refs
    rows, tile = own_panels.shape[1:]
    chip_blocks = 2 * rows // tile
    chip, core = place()

    def write(other_panels):
        def transposed(at):
            return chip_q[pl.ds(pl.multiple_of(at * rows, rows), rows), :].T

        own_t, other_t = transposed(core), transposed(1 - core)

        def mirrored(first, blocks):
            return mirrored_blocks(
                [(own_t, own_panels, first), (other_t, other_panels, first)], blocks
            )

        q = split(chip_q[...].astype(jnp.float32), tile)
        for k, message in zip(slots, messages, strict=True):
            cls = class_of(k, core, in_lower_half(chips), chip % 2, chips)
            up = chip < (chip ^ cls)
            blocks = mirrored(cls // 2 * chip_blocks, chip_blocks)
            write_message(
                message, [jnp.where(up, m, x) for m, x in zip(blocks, q, strict=True)]
            )
        half = chip_blocks // 2
        last = other_panels.shape[0] - 1 - chip_blocks
        local = mirrored(last + core * half, half)
        for b, m in enumerate(local):
            mirror[b * tile:(b + 1) * tile, :] = m

    @pl.when(in_lower_half(chips))
    def _():
        write(far_panels)

    @pl.when(jnp.logical_not(in_lower_half(chips)))
    def _():
        copies = fetch(sems, (index_ref, index), (count_ref, count))
        panels[...] = jnp.zeros_like(panels)
        for copy in copies:
            copy.wait()
        put_tiles(index, count, tiles, panels, chip_blocks)
        write(panels)


def class_of(k, core, from_lower, odd, chips):
    if k < chips // 4:
        return 2 * k + core
    other = chips // 2 + chips // 4 - 1 - k
    if isinstance(core, int):
        turned = not odd if from_lower else odd and core == 0
        return 2 * (other if turned else k) + core
    turned = jnp.where(from_lower, odd == 0, (odd == 1) & (core == 0))
    return 2 * jnp.where(turned, other, k) + core


def is_low(chips, k, mine):
    chip, core = place()
    carrier = core if mine else 1 - core
    odd = (chip + carrier) % 2
    cls = class_of(k, carrier, jnp.logical_not(in_lower_half(chips)), odd, chips)
    return (chip ^ cls) < chip, cls


def own_half(blocks):
    _, core = place()
    half = len(blocks) // 2
    return [
        jnp.where(core == 0, a, b)
        for a, b in zip(blocks[:half], blocks[half:], strict=True)
    ]


def gather_part(chips, sources, rows_panels, direct, mirror, messages):
    total = direct[...]
    mirrored = split(mirror[...], rows_panels.shape[2])
    for (k, mine), message in zip(sources, messages, strict=True):
        low, cls = is_low(chips, k, mine)
        blocks = read_message(message)
        total = total + direct_sum(rows_panels, cls * len(blocks), blocks)
        mirrored = [
            m + jnp.where(low, x, 0.0)
            for m, x in zip(mirrored, own_half(blocks), strict=True)
        ]
    return total, mirrored


def gather_kernel(chips, sources, rows_panels, direct, mirror, *refs):
    *messages, direct_out, mirror_out = refs
    tile = rows_panels.shape[2]
    total, mirrored = gather_part(chips, sources, rows_panels, direct, mirror, messages)
    direct_out[...] = total
    for b, m in enumerate(mirrored):
        mirror_out[b * tile:(b + 1) * tile, :] = m


def join_kernel(chips, sources, rows_panels, direct, mirror, *refs):
    *messages, base = refs
    tile = rows_panels.shape[2]
    total, mirrored = gather_part(chips, sources, rows_panels, direct, mirror, messages)
    for b, (block, m) in enumerate(zip(split(total, tile), mirrored, strict=True)):
        base[b * tile:(b + 1) * tile, :] = block + m.T


def final_kernel(chips, k, factor, rows_panels, base, message, out, result, sem):
    tile = rows_panels.shape[2]
    low, cls = is_low(chips, k, False)

    @pl.when(low)
    def _():
        for b, x in enumerate(own_half(read_message(message))):
            at = slice(b * tile, (b + 1) * tile)
            result[at, :] = (base[at, :] + x.T) * factor

    @pl.when(jnp.logical_not(low))
    def _():
        blocks = read_message(message)
        total = direct_sum(rows_panels, cls * len(blocks), blocks)
        result[...] = (base[...] + total) * factor

    copy = pltpu.make_async_copy(result, out, sem)
    copy.start()
    copy.wait()


VMEM = functools.partial(pl.BlockSpec, memory_space=pltpu.VMEM)
SMEM = functools.partial(pl.BlockSpec, memory_space=pltpu.SMEM)


def on_device(devices, tile_blocks, q_block, tile_index, tile_count):
    tile = tile_blocks.shape[1]
    rows, columns = q_block.shape
    chips = devices // 2
    slots = chips // 2
    chip_rows = 2 * rows
    chip_blocks = chip_rows // tile
    wide = jnp.float32
    other_core = [(d, d ^ 1) for d in range(devices)]

    def swap(x):
        return lax.ppermute(x, "row", other_core)

    index = tile_index.T
    other_tiles = swap(tile_blocks)
    other_q = swap(q_block)
    other_index = swap(index)
    other_count = swap(tile_count)

    panels_shape = jax.ShapeDtypeStruct(
        ((slots + 1) * chip_blocks + 1, rows, tile), jnp.bfloat16
    )
    rows_panels_shape = jax.ShapeDtypeStruct(
        (chips * chip_blocks, rows, tile), jnp.bfloat16
    )
    q_shape = jax.ShapeDtypeStruct((chip_rows, columns), jnp.bfloat16)
    message = jax.ShapeDtypeStruct((chip_rows + 16, columns), jnp.int16)
    half_shape = jax.ShapeDtypeStruct((rows, columns), wide)
    params = pltpu.CompilerParams(vmem_limit_bytes=48 * 2**20)
    hbm = pl.BlockSpec(memory_space=pltpu.HBM)
    own = [
        pltpu.with_memory_space_constraint(a, pltpu.HBM)
        for a in (index, tile_count, tile_blocks)
    ]
    own_scratch = [
        pltpu.SMEM(index.shape, index.dtype),
        pltpu.SMEM(tile_count.shape, tile_count.dtype),
        pltpu.VMEM(tile_blocks.shape, tile_blocks.dtype),
        pltpu.SemaphoreType.DMA((3,)),
    ]
    own_panels = pl.pallas_call(
        own_kernel,
        out_shape=panels_shape,
        in_specs=[hbm] * 3,
        out_specs=VMEM(),
        scratch_shapes=own_scratch,
        compiler_params=params,
        name="own_tiles",
    )(*own)
    far = list(range(slots // 2, slots))
    near = list(reversed(range(slots // 2)))
    rest = near + far[1:]
    other = (other_index, other_count, other_tiles)
    other_specs = [pl.BlockSpec(memory_space=pl.ANY)] * 2 + [VMEM()]
    other_scratch = [*own_scratch[:2], pltpu.SemaphoreType.DMA((2,))]
    chip_q, far_message, far_panels = pl.pallas_call(
        functools.partial(far_kernel, chips, far[0]),
        out_shape=[q_shape, message, panels_shape],
        in_specs=other_specs + [VMEM()] * 3,
        out_specs=[VMEM()] * 3,
        scratch_shapes=[pltpu.VMEM((chip_blocks, tile, columns), wide), *other_scratch],
        compiler_params=params,
        name="pack_far",
    )(*other, q_block, other_q, own_panels)
    *rest_messages, mirror = pl.pallas_call(
        functools.partial(near_kernel, chips, rest),
        out_shape=[message] * len(rest) + [half_shape],
        in_specs=other_specs + [VMEM()] * 3,
        out_specs=[VMEM()] * (len(rest) + 1),
        scratch_shapes=[pltpu.VMEM(panels_shape.shape, jnp.bfloat16), *other_scratch],
        compiler_params=params,
        name="pack_near",
    )(*other, own_panels, far_panels, chip_q)
    messages = dict(zip(far[:1] + rest, [far_message, *rest_messages], strict=True))
    received = {
        k: lax.ppermute(messages[k], "row", [
            (d, d ^ (2 * cls))
            for d in range(devices)
            if (cls := class_of(k, d % 2, d < devices // 2, d // 2 % 2, chips))
        ])
        for k in far[:1] + rest
    }

    rows_panels, direct = pl.pallas_call(
        direct_kernel,
        out_shape=[rows_panels_shape, half_shape],
        in_specs=[hbm] * 3 + [VMEM()],
        out_specs=[VMEM()] * 2,
        scratch_shapes=own_scratch,
        compiler_params=params,
        cost_estimate=pl.CostEstimate(
            flops=10**10, bytes_accessed=0, transcendentals=0
        ),
        name="direct_local",
    )(*own, chip_q)

    def gather(kernel, sources, sums, name, outs, passed=()):
        sums = list(sums)
        return pl.pallas_call(
            functools.partial(kernel, chips, sources),
            out_shape=[half_shape] * outs + [message] * len(passed),
            in_specs=[VMEM()] * (1 + len(sums) + len(sources) + len(passed)),
            out_specs=[VMEM()] * (outs + len(passed)),
            input_output_aliases={
                1 + len(sums) + len(sources) + n: outs + n for n in range(len(passed))
            },
            compiler_params=params,
            cost_estimate=pl.CostEstimate(
                flops=10**10, bytes_accessed=0, transcendentals=0
            ),
            name=name,
        )(rows_panels, *sums,
          *((received if mine else other)[k] for k, mine in sources), *passed)

    *late, last = near + far[1:]
    other = {k: swap(received[k]) for k in [far[0], *late, last]}
    direct, mirror = gather(
        gather_kernel, [(far[0], True), (far[0], False)], (direct, mirror),
        "gather_first", 2,
    )
    (base,) = gather(
        join_kernel,
        [(k, mine) for k in late for mine in (True, False)] + [(last, True)],
        (direct, mirror), "gather_most", 1,
    )
    return pl.pallas_call(
        functools.partial(final_kernel, chips, last, 1.0 / math.sqrt(rows * devices)),
        out_shape=half_shape,
        in_specs=[VMEM()] * 3,
        out_specs=hbm,
        scratch_shapes=[pltpu.VMEM((rows, columns), wide), pltpu.SemaphoreType.DMA(())],
        compiler_params=params,
        name="gather_last",
    )(rows_panels, base, other[last])


def solution(mesh):
    return jax.shard_map(
        functools.partial(on_device, mesh.shape["row"]),
        mesh=mesh,
        in_specs=(
            P(("grp", "row"), None, None),
            P(("grp", "row"), None),
            P(("grp", "row"), None),
            P(("grp", "row")),
        ),
        out_specs=P(("grp", "row"), None),
        check_vma=False,
    )
```

```python
import functools
import math

import jax
import jax.numpy as jnp
from jax import lax
from jax.experimental import pallas as pl
from jax.experimental.pallas import tpu as pltpu
from jax.sharding import PartitionSpec as P

TOP = 32700.0
STEPS = 16.0
LEAST = 1e-30


def place():
    me = lax.axis_index("row")
    return me // 2, me % 2


def scale_of(code):
    return jnp.exp2(code * (1.0 / STEPS))


def encode(x):
    top = jnp.maximum(jnp.max(jnp.abs(x), axis=0, keepdims=True), LEAST)
    code = jnp.ceil(jnp.log2(top) * STEPS)
    values = jnp.round(x * (TOP / scale_of(code)))
    return values.astype(jnp.int32).astype(jnp.int16), code


def live_tiles(count):
    live = count[0]
    for r in range(1, count.shape[0]):
        live = live + count[r]
    return live


def put_tiles(index, count, tiles, panels, chip_blocks):
    chip, core = place()
    tile = tiles.shape[1]
    spare = panels.shape[0] - 1
    local = spare // chip_blocks - 1
    step = 2 if tiles.shape[0] % 2 == 0 else 1
    live = live_tiles(count)

    def put(n, carry):
        for s in [n * step + e for e in range(step)]:
            i, j = index[0, s], index[1, s]
            cls = chip ^ (j // chip_blocks)
            slot = jnp.where(cls == 0, local, cls // 2)
            wanted = (s < live) & ((cls == 0) | (cls % 2 == core))
            panel = jnp.where(wanted, slot * chip_blocks + j % chip_blocks, spare)
            at = pl.multiple_of((i % (chip_blocks // 2)) * tile, tile)
            panels[panel, pl.ds(at, tile), :] = tiles[s]
        return carry

    lax.fori_loop(0, (live + step - 1) // step, put, 0)


def fetch(sems, *pairs):
    copies = [
        pltpu.make_async_copy(a, b, sems.at[n]) for n, (a, b) in enumerate(pairs)
    ]
    for copy in copies:
        copy.start()
    return copies


def own_kernel(index_ref, count_ref, tiles_ref, panels, index, count, tiles, sems):
    copies = fetch(sems, (index_ref, index), (count_ref, count), (tiles_ref, tiles))
    panels[...] = jnp.zeros_like(panels)
    for copy in copies:
        copy.wait()
    put_tiles(index, count, tiles, panels, 2 * panels.shape[1] // panels.shape[2])


def direct_kernel(
    index_ref, count_ref, tiles_ref, chip_q, rows_panels, direct,
    index, count, tiles, sems,
):
    copies = fetch(sems, (index_ref, index), (count_ref, count), (tiles_ref, tiles))
    rows_panels[...] = jnp.zeros_like(rows_panels)
    for copy in copies:
        copy.wait()
    tile = tiles.shape[1]
    rows = rows_panels.shape[1]
    chip_blocks = 2 * rows // tile
    chip, _ = place()

    def put(s, carry):
        i, j = index[0, s], index[1, s]
        panel = (chip ^ (j // chip_blocks)) * chip_blocks + j % chip_blocks
        at = pl.multiple_of((i % (rows // tile)) * tile, tile)
        rows_panels[panel, pl.ds(at, tile), :] = tiles[s]
        return carry

    lax.fori_loop(0, live_tiles(count), put, 0)
    direct[...] = direct_sum(rows_panels, 0, split(chip_q[...], tile))


def write_message(message, blocks):
    tile = message.shape[1]
    codes = []
    for b, x in enumerate(blocks):
        values, code = encode(x)
        message[b * tile:(b + 1) * tile, :] = values
        codes.append(code)
    which = lax.broadcasted_iota(jnp.int32, (16, tile), 0)
    tail = jnp.zeros((16, tile), jnp.float32)
    for b, code in enumerate(codes):
        tail = jnp.where(which == b, code, tail)
    message[len(blocks) * tile:, :] = tail.astype(jnp.int32).astype(jnp.int16)


def read_message(message):
    tile = message.shape[1]
    blocks = message.shape[0] // tile
    tail = message[blocks * tile:, :].astype(jnp.int32).astype(jnp.float32)
    scales = scale_of(tail) * (1.0 / TOP)
    return [
        message[b * tile:(b + 1) * tile, :].astype(jnp.int32).astype(jnp.float32)
        * scales[b:b + 1, :]
        for b in range(blocks)
    ]


def mirrored_blocks(parts, blocks):
    tile = parts[0][1].shape[2]
    sums = []
    for b in range(0, blocks, 2):
        pair = sum(
            jnp.dot(
                q_t,
                jnp.concatenate([panels[g + b], panels[g + b + 1]], axis=1),
                preferred_element_type=jnp.float32,
            )
            for q_t, panels, g in parts
        )
        sums += [pair[:, :tile], pair[:, tile:]]
    return sums


def direct_sum(panels, start, blocks):
    total = None
    for b in range(0, len(blocks), 2):
        pair = jnp.concatenate([panels[start + b], panels[start + b + 1]], axis=1)
        q = jnp.concatenate(blocks[b:b + 2], axis=0).astype(jnp.bfloat16)
        part = jnp.dot(pair, q, preferred_element_type=jnp.float32)
        total = part if total is None else total + part
    return total


def split(x, tile):
    return [x[at:at + tile, :] for at in range(0, x.shape[0], tile)]


def in_lower_half(chips):
    return place()[0] < chips // 2


def far_kernel(
    chips, k, index_ref, count_ref, tiles, own_q, other_q, own_panels,
    chip_q, message, panels, sums, index, count, sems,
):
    rows, tile = own_q.shape[0], tiles.shape[1]
    chip_blocks = 2 * rows // tile
    chip, core = place()
    chip_q[pl.ds(pl.multiple_of(core * rows, rows), rows), :] = own_q[...]
    chip_q[pl.ds(pl.multiple_of((1 - core) * rows, rows), rows), :] = other_q[...]

    @pl.when(in_lower_half(chips))
    def _():
        copies = fetch(sems, (index_ref, index), (count_ref, count))
        panels[...] = jnp.zeros_like(panels)
        first = class_of(k, core, True, chip % 2, chips) // 2 * chip_blocks
        mine = mirrored_blocks([(own_q[...].T, own_panels, first)], chip_blocks)
        for b, m in enumerate(mine):
            sums[b] = m
        other_t = other_q[...].T
        for copy in copies:
            copy.wait()
        put_tiles(index, count, tiles, panels, chip_blocks)
        theirs = mirrored_blocks([(other_t, panels, first)], chip_blocks)
        write_message(message, [sums[b] + m for b, m in enumerate(theirs)])

    @pl.when(jnp.logical_not(in_lower_half(chips)))
    def _():
        write_message(message, split(chip_q[...].astype(jnp.float32), tile))


def near_kernel(
    chips, slots, index_ref, count_ref, tiles, own_panels, far_panels, chip_q,
    far_message, *refs
):
    *messages, mirror, panels, index, count, sems = refs
    rows, tile = own_panels.shape[1:]
    chip_blocks = 2 * rows // tile
    chip, core = place()

    def write(other_panels, upper):
        def transposed(at):
            return chip_q[pl.ds(pl.multiple_of(at * rows, rows), rows), :].T

        own_t, other_t = transposed(core), transposed(1 - core)

        def mirrored(first, blocks):
            return mirrored_blocks(
                [(own_t, own_panels, first), (other_t, other_panels, first)], blocks
            )

        q = split(chip_q[...].astype(jnp.float32), tile)
        for k, message in zip(slots, messages, strict=True):
            if upper and k >= chips // 4:
                message[...] = far_message[...]
                continue
            cls = class_of(k, core, in_lower_half(chips), chip % 2, chips)
            up = chip < (chip ^ cls)
            blocks = mirrored(cls // 2 * chip_blocks, chip_blocks)
            write_message(
                message, [jnp.where(up, m, x) for m, x in zip(blocks, q, strict=True)]
            )
        half = chip_blocks // 2
        last = other_panels.shape[0] - 1 - chip_blocks
        local = mirrored(last + core * half, half)
        for b, m in enumerate(local):
            mirror[b * tile:(b + 1) * tile, :] = m

    @pl.when(in_lower_half(chips))
    def _():
        write(far_panels, False)

    @pl.when(jnp.logical_not(in_lower_half(chips)))
    def _():
        copies = fetch(sems, (index_ref, index), (count_ref, count))
        panels[...] = jnp.zeros_like(panels)
        for copy in copies:
            copy.wait()
        put_tiles(index, count, tiles, panels, chip_blocks)
        write(panels, True)


def class_of(k, core, from_lower, odd, chips):
    if k < chips // 4:
        return 2 * k + core
    other = chips // 2 + chips // 4 - 1 - k
    if isinstance(core, int):
        turned = not odd if from_lower else odd and core == 0
        return 2 * (other if turned else k) + core
    turned = jnp.where(from_lower, odd == 0, (odd == 1) & (core == 0))
    return 2 * jnp.where(turned, other, k) + core


def is_low(chips, k, mine):
    chip, core = place()
    carrier = core if mine else 1 - core
    odd = (chip + carrier) % 2
    cls = class_of(k, carrier, jnp.logical_not(in_lower_half(chips)), odd, chips)
    return (chip ^ cls) < chip, cls


def own_half(blocks):
    _, core = place()
    half = len(blocks) // 2
    return [
        jnp.where(core == 0, a, b)
        for a, b in zip(blocks[:half], blocks[half:], strict=True)
    ]


def gather_part(chips, sources, rows_panels, direct, mirror, messages):
    total = direct[...]
    mirrored = split(mirror[...], rows_panels.shape[2])
    for (k, mine), message in zip(sources, messages, strict=True):
        low, cls = is_low(chips, k, mine)
        blocks = read_message(message)
        total = total + direct_sum(rows_panels, cls * len(blocks), blocks)
        mirrored = [
            m + jnp.where(low, x, 0.0)
            for m, x in zip(mirrored, own_half(blocks), strict=True)
        ]
    return total, mirrored


def gather_kernel(chips, sources, rows_panels, direct, mirror, *refs):
    *messages, direct_out, mirror_out = refs
    tile = rows_panels.shape[2]
    total, mirrored = gather_part(chips, sources, rows_panels, direct, mirror, messages)
    direct_out[...] = total
    for b, m in enumerate(mirrored):
        mirror_out[b * tile:(b + 1) * tile, :] = m


def join_kernel(chips, sources, rows_panels, direct, mirror, *refs):
    *messages, base = refs
    tile = rows_panels.shape[2]
    total, mirrored = gather_part(chips, sources, rows_panels, direct, mirror, messages)
    for b, (block, m) in enumerate(zip(split(total, tile), mirrored, strict=True)):
        base[b * tile:(b + 1) * tile, :] = block + m.T


def final_kernel(chips, k, factor, rows_panels, base, message, out, result, sem):
    tile = rows_panels.shape[2]
    low, cls = is_low(chips, k, False)

    @pl.when(low)
    def _():
        for b, x in enumerate(own_half(read_message(message))):
            at = slice(b * tile, (b + 1) * tile)
            result[at, :] = (base[at, :] + x.T) * factor

    @pl.when(jnp.logical_not(low))
    def _():
        blocks = read_message(message)
        total = direct_sum(rows_panels, cls * len(blocks), blocks)
        result[...] = (base[...] + total) * factor

    copy = pltpu.make_async_copy(result, out, sem)
    copy.start()
    copy.wait()


VMEM = functools.partial(pl.BlockSpec, memory_space=pltpu.VMEM)
SMEM = functools.partial(pl.BlockSpec, memory_space=pltpu.SMEM)


def on_device(devices, tile_blocks, q_block, tile_index, tile_count):
    tile = tile_blocks.shape[1]
    rows, columns = q_block.shape
    chips = devices // 2
    slots = chips // 2
    chip_rows = 2 * rows
    chip_blocks = chip_rows // tile
    wide = jnp.float32
    other_core = [(d, d ^ 1) for d in range(devices)]

    def swap(x):
        return lax.ppermute(x, "row", other_core)

    index = tile_index.T
    other_tiles = swap(tile_blocks)
    other_q = swap(q_block)
    other_index = swap(index)
    other_count = swap(tile_count)

    panels_shape = jax.ShapeDtypeStruct(
        ((slots + 1) * chip_blocks + 1, rows, tile), jnp.bfloat16
    )
    rows_panels_shape = jax.ShapeDtypeStruct(
        (chips * chip_blocks, rows, tile), jnp.bfloat16
    )
    q_shape = jax.ShapeDtypeStruct((chip_rows, columns), jnp.bfloat16)
    message = jax.ShapeDtypeStruct((chip_rows + 16, columns), jnp.int16)
    half_shape = jax.ShapeDtypeStruct((rows, columns), wide)
    params = pltpu.CompilerParams(vmem_limit_bytes=48 * 2**20)
    hbm = pl.BlockSpec(memory_space=pltpu.HBM)
    own = [
        pltpu.with_memory_space_constraint(a, pltpu.HBM)
        for a in (index, tile_count, tile_blocks)
    ]
    own_scratch = [
        pltpu.SMEM(index.shape, index.dtype),
        pltpu.SMEM(tile_count.shape, tile_count.dtype),
        pltpu.VMEM(tile_blocks.shape, tile_blocks.dtype),
        pltpu.SemaphoreType.DMA((3,)),
    ]
    own_panels = pl.pallas_call(
        own_kernel,
        out_shape=panels_shape,
        in_specs=[hbm] * 3,
        out_specs=VMEM(),
        scratch_shapes=own_scratch,
        compiler_params=params,
        name="own_tiles",
    )(*own)
    far = list(range(slots // 2, slots))
    near = list(reversed(range(slots // 2)))
    rest = near + far[1:]
    other = (other_index, other_count, other_tiles)
    other_specs = [pl.BlockSpec(memory_space=pl.ANY)] * 2 + [VMEM()]
    other_scratch = [*own_scratch[:2], pltpu.SemaphoreType.DMA((2,))]
    chip_q, far_message, far_panels = pl.pallas_call(
        functools.partial(far_kernel, chips, far[0]),
        out_shape=[q_shape, message, panels_shape],
        in_specs=other_specs + [VMEM()] * 3,
        out_specs=[VMEM()] * 3,
        scratch_shapes=[pltpu.VMEM((chip_blocks, tile, columns), wide), *other_scratch],
        compiler_params=params,
        name="pack_far",
    )(*other, q_block, other_q, own_panels)
    *rest_messages, mirror = pl.pallas_call(
        functools.partial(near_kernel, chips, rest),
        out_shape=[message] * len(rest) + [half_shape],
        in_specs=other_specs + [VMEM()] * 4,
        out_specs=[VMEM()] * (len(rest) + 1),
        scratch_shapes=[pltpu.VMEM(panels_shape.shape, jnp.bfloat16), *other_scratch],
        compiler_params=params,
        name="pack_near",
    )(*other, own_panels, far_panels, chip_q, far_message)
    messages = dict(zip(far[:1] + rest, [far_message, *rest_messages], strict=True))
    received = {
        k: lax.ppermute(messages[k], "row", [
            (d, d ^ (2 * cls))
            for d in range(devices)
            if (cls := class_of(k, d % 2, d < devices // 2, d // 2 % 2, chips))
        ])
        for k in far[:1] + rest
    }

    rows_panels, direct = pl.pallas_call(
        direct_kernel,
        out_shape=[rows_panels_shape, half_shape],
        in_specs=[hbm] * 3 + [VMEM()],
        out_specs=[VMEM()] * 2,
        scratch_shapes=own_scratch,
        compiler_params=params,
        cost_estimate=pl.CostEstimate(
            flops=10**10, bytes_accessed=0, transcendentals=0
        ),
        name="direct_local",
    )(*own, chip_q)

    def gather(kernel, sources, sums, name, outs, passed=()):
        sums = list(sums)
        return pl.pallas_call(
            functools.partial(kernel, chips, sources),
            out_shape=[half_shape] * outs + [message] * len(passed),
            in_specs=[VMEM()] * (1 + len(sums) + len(sources) + len(passed)),
            out_specs=[VMEM()] * (outs + len(passed)),
            input_output_aliases={
                1 + len(sums) + len(sources) + n: outs + n for n in range(len(passed))
            },
            compiler_params=params,
            cost_estimate=pl.CostEstimate(
                flops=10**10, bytes_accessed=0, transcendentals=0
            ),
            name=name,
        )(rows_panels, *sums,
          *((received if mine else other)[k] for k, mine in sources), *passed)

    *late, last = near + far[1:]
    other = {k: swap(received[k]) for k in [far[0], *late, last]}
    direct, mirror = gather(
        gather_kernel, [(far[0], True), (far[0], False)], (direct, mirror),
        "gather_first", 2,
    )
    (base,) = gather(
        join_kernel,
        [(k, mine) for k in late for mine in (True, False)] + [(last, True)],
        (direct, mirror), "gather_most", 1,
    )
    return pl.pallas_call(
        functools.partial(final_kernel, chips, last, 1.0 / math.sqrt(rows * devices)),
        out_shape=half_shape,
        in_specs=[VMEM()] * 3,
        out_specs=hbm,
        scratch_shapes=[pltpu.VMEM((rows, columns), wide), pltpu.SemaphoreType.DMA(())],
        compiler_params=params,
        name="gather_last",
    )(rows_panels, base, other[last])


def solution(mesh):
    return jax.shard_map(
        functools.partial(on_device, mesh.shape["row"]),
        mesh=mesh,
        in_specs=(
            P(("grp", "row"), None, None),
            P(("grp", "row"), None),
            P(("grp", "row"), None),
            P(("grp", "row")),
        ),
        out_specs=P(("grp", "row"), None),
        check_vma=False,
    )
```

```python
import functools
import math

import jax
import jax.numpy as jnp
from jax import lax
from jax.experimental import pallas as pl
from jax.experimental.pallas import tpu as pltpu
from jax.sharding import PartitionSpec as P

TOP = 32700.0
STEPS = 16.0
LEAST = 1e-30


def place():
    me = lax.axis_index("row")
    return me // 2, me % 2


def scale_of(code):
    return jnp.exp2(code * (1.0 / STEPS))


def encode(x):
    top = jnp.maximum(jnp.max(jnp.abs(x), axis=0, keepdims=True), LEAST)
    code = jnp.ceil(jnp.log2(top) * STEPS)
    values = jnp.round(x * (TOP / scale_of(code)))
    return values.astype(jnp.int32).astype(jnp.int16), code


def live_tiles(count):
    live = count[0]
    for r in range(1, count.shape[0]):
        live = live + count[r]
    return live


def put_tiles(index, count, tiles, panels, chip_blocks):
    chip, core = place()
    tile = tiles.shape[1]
    spare = panels.shape[0] - 1
    local = spare // chip_blocks - 1
    step = 2 if tiles.shape[0] % 2 == 0 else 1
    live = live_tiles(count)

    def put(n, carry):
        for s in [n * step + e for e in range(step)]:
            i, j = index[0, s], index[1, s]
            cls = chip ^ (j // chip_blocks)
            slot = jnp.where(cls == 0, local, cls // 2)
            wanted = (s < live) & ((cls == 0) | (cls % 2 == core))
            panel = jnp.where(wanted, slot * chip_blocks + j % chip_blocks, spare)
            at = pl.multiple_of((i % (chip_blocks // 2)) * tile, tile)
            panels[panel, pl.ds(at, tile), :] = tiles[s]
        return carry

    lax.fori_loop(0, (live + step - 1) // step, put, 0)


def fetch(sems, *pairs):
    copies = [
        pltpu.make_async_copy(a, b, sems.at[n]) for n, (a, b) in enumerate(pairs)
    ]
    for copy in copies:
        copy.start()
    return copies


def own_kernel(index_ref, count_ref, tiles_ref, panels, index, count, tiles, sems):
    copies = fetch(sems, (index_ref, index), (count_ref, count), (tiles_ref, tiles))
    panels[...] = jnp.zeros_like(panels)
    for copy in copies:
        copy.wait()
    put_tiles(index, count, tiles, panels, 2 * panels.shape[1] // panels.shape[2])


def direct_kernel(
    index_ref, count_ref, tiles_ref, chip_q, rows_panels, direct,
    index, count, tiles, sems,
):
    copies = fetch(sems, (index_ref, index), (count_ref, count), (tiles_ref, tiles))
    rows_panels[...] = jnp.zeros_like(rows_panels)
    for copy in copies:
        copy.wait()
    tile = tiles.shape[1]
    rows = rows_panels.shape[1]
    chip_blocks = 2 * rows // tile
    chip, _ = place()

    def put(s, carry):
        i, j = index[0, s], index[1, s]
        panel = (chip ^ (j // chip_blocks)) * chip_blocks + j % chip_blocks
        at = pl.multiple_of((i % (rows // tile)) * tile, tile)
        rows_panels[panel, pl.ds(at, tile), :] = tiles[s]
        return carry

    lax.fori_loop(0, live_tiles(count), put, 0)
    direct[...] = direct_sum(rows_panels, 0, split(chip_q[...], tile))


def write_message(message, blocks):
    tile = message.shape[1]
    codes = []
    for b, x in enumerate(blocks):
        values, code = encode(x)
        message[b * tile:(b + 1) * tile, :] = values
        codes.append(code)
    which = lax.broadcasted_iota(jnp.int32, (16, tile), 0)
    tail = jnp.zeros((16, tile), jnp.float32)
    for b, code in enumerate(codes):
        tail = jnp.where(which == b, code, tail)
    message[len(blocks) * tile:, :] = tail.astype(jnp.int32).astype(jnp.int16)


def read_message(message):
    tile = message.shape[1]
    blocks = message.shape[0] // tile
    tail = message[blocks * tile:, :].astype(jnp.int32).astype(jnp.float32)
    scales = scale_of(tail) * (1.0 / TOP)
    return [
        message[b * tile:(b + 1) * tile, :].astype(jnp.int32).astype(jnp.float32)
        * scales[b:b + 1, :]
        for b in range(blocks)
    ]


def mirrored_blocks(parts, blocks):
    tile = parts[0][1].shape[2]
    sums = []
    for b in range(0, blocks, 2):
        pair = sum(
            jnp.dot(
                q_t,
                jnp.concatenate([panels[g + b], panels[g + b + 1]], axis=1),
                preferred_element_type=jnp.float32,
            )
            for q_t, panels, g in parts
        )
        sums += [pair[:, :tile], pair[:, tile:]]
    return sums


def direct_sum(panels, start, blocks):
    total = None
    for b in range(0, len(blocks), 2):
        pair = jnp.concatenate([panels[start + b], panels[start + b + 1]], axis=1)
        q = jnp.concatenate(blocks[b:b + 2], axis=0).astype(jnp.bfloat16)
        part = jnp.dot(pair, q, preferred_element_type=jnp.float32)
        total = part if total is None else total + part
    return total


def split(x, tile):
    return [x[at:at + tile, :] for at in range(0, x.shape[0], tile)]


def in_lower_half(chips):
    return place()[0] < chips // 2


def far_kernel(
    chips, k, index_ref, count_ref, tiles, own_q, other_q, own_panels,
    chip_q, message, panels, sums, index, count, sems,
):
    rows, tile = own_q.shape[0], tiles.shape[1]
    chip_blocks = 2 * rows // tile
    chip, core = place()

    def keep_q():
        chip_q[pl.ds(pl.multiple_of(core * rows, rows), rows), :] = own_q[...]
        chip_q[pl.ds(pl.multiple_of((1 - core) * rows, rows), rows), :] = other_q[...]

    @pl.when(in_lower_half(chips))
    def _():
        copies = fetch(sems, (index_ref, index), (count_ref, count))
        keep_q()
        panels[...] = jnp.zeros_like(panels)
        first = class_of(k, core, True, chip % 2, chips) // 2 * chip_blocks
        mine = mirrored_blocks([(own_q[...].T, own_panels, first)], chip_blocks)
        for b, m in enumerate(mine):
            sums[b] = m
        other_t = other_q[...].T
        for copy in copies:
            copy.wait()
        put_tiles(index, count, tiles, panels, chip_blocks)
        theirs = mirrored_blocks([(other_t, panels, first)], chip_blocks)
        write_message(message, [sums[b] + m for b, m in enumerate(theirs)])

    @pl.when(jnp.logical_not(in_lower_half(chips)))
    def _():
        keep_q()
        write_message(message, split(chip_q[...].astype(jnp.float32), tile))


def near_kernel(
    chips, slots, index_ref, count_ref, tiles, own_panels, far_panels, chip_q, *refs
):
    *messages, mirror, panels, index, count, sems = refs
    rows, tile = own_panels.shape[1:]
    chip_blocks = 2 * rows // tile
    chip, core = place()

    def write(other_panels):
        def transposed(at):
            return chip_q[pl.ds(pl.multiple_of(at * rows, rows), rows), :].T

        own_t, other_t = transposed(core), transposed(1 - core)

        def mirrored(first, blocks):
            return mirrored_blocks(
                [(own_t, own_panels, first), (other_t, other_panels, first)], blocks
            )

        q = split(chip_q[...].astype(jnp.float32), tile)
        for k, message in zip(slots, messages, strict=True):
            cls = class_of(k, core, in_lower_half(chips), chip % 2, chips)
            up = chip < (chip ^ cls)
            blocks = mirrored(cls // 2 * chip_blocks, chip_blocks)
            write_message(
                message, [jnp.where(up, m, x) for m, x in zip(blocks, q, strict=True)]
            )
        half = chip_blocks // 2
        last = other_panels.shape[0] - 1 - chip_blocks
        local = mirrored(last + core * half, half)
        for b, m in enumerate(local):
            mirror[b * tile:(b + 1) * tile, :] = m

    @pl.when(in_lower_half(chips))
    def _():
        write(far_panels)

    @pl.when(jnp.logical_not(in_lower_half(chips)))
    def _():
        copies = fetch(sems, (index_ref, index), (count_ref, count))
        panels[...] = jnp.zeros_like(panels)
        for copy in copies:
            copy.wait()
        put_tiles(index, count, tiles, panels, chip_blocks)
        write(panels)


def class_of(k, core, from_lower, odd, chips):
    if k < chips // 4:
        return 2 * k + core
    other = chips // 2 + chips // 4 - 1 - k
    if isinstance(core, int):
        turned = not odd if from_lower else odd and core == 0
        return 2 * (other if turned else k) + core
    turned = jnp.where(from_lower, odd == 0, (odd == 1) & (core == 0))
    return 2 * jnp.where(turned, other, k) + core


def is_low(chips, k, mine):
    chip, core = place()
    carrier = core if mine else 1 - core
    odd = (chip + carrier) % 2
    cls = class_of(k, carrier, jnp.logical_not(in_lower_half(chips)), odd, chips)
    return (chip ^ cls) < chip, cls


def own_half(blocks):
    _, core = place()
    half = len(blocks) // 2
    return [
        jnp.where(core == 0, a, b)
        for a, b in zip(blocks[:half], blocks[half:], strict=True)
    ]


def gather_part(chips, sources, rows_panels, direct, mirror, messages):
    total = direct[...]
    mirrored = split(mirror[...], rows_panels.shape[2])
    for (k, mine), message in zip(sources, messages, strict=True):
        low, cls = is_low(chips, k, mine)
        blocks = read_message(message)
        total = total + direct_sum(rows_panels, cls * len(blocks), blocks)
        mirrored = [
            m + jnp.where(low, x, 0.0)
            for m, x in zip(mirrored, own_half(blocks), strict=True)
        ]
    return total, mirrored


def gather_kernel(chips, sources, rows_panels, direct, mirror, *refs):
    *messages, direct_out, mirror_out = refs
    tile = rows_panels.shape[2]
    total, mirrored = gather_part(chips, sources, rows_panels, direct, mirror, messages)
    direct_out[...] = total
    for b, m in enumerate(mirrored):
        mirror_out[b * tile:(b + 1) * tile, :] = m


def join_kernel(chips, sources, rows_panels, direct, mirror, *refs):
    *messages, base = refs
    tile = rows_panels.shape[2]
    total, mirrored = gather_part(chips, sources, rows_panels, direct, mirror, messages)
    for b, (block, m) in enumerate(zip(split(total, tile), mirrored, strict=True)):
        base[b * tile:(b + 1) * tile, :] = block + m.T


def final_kernel(chips, k, factor, rows_panels, base, message, out, result, sems):
    tile = rows_panels.shape[2]
    low, cls = is_low(chips, k, False)
    parts = [pl.ds(at, tile) for at in range(0, result.shape[0], tile)]
    copies = [
        pltpu.make_async_copy(result.at[at], out.at[at], sems.at[n])
        for n, at in enumerate(parts)
    ]

    @pl.when(low)
    def _():
        blocks = own_half(read_message(message))
        for at, x, copy in zip(parts, blocks, copies, strict=True):
            result[at, :] = (base[at, :] + x.T) * factor
            copy.start()

    @pl.when(jnp.logical_not(low))
    def _():
        blocks = read_message(message)
        q = jnp.concatenate(blocks, axis=0).astype(jnp.bfloat16)
        for at, copy in zip(parts, copies, strict=True):
            row = jnp.concatenate(
                [rows_panels[cls * len(blocks) + b, at, :] for b in range(len(blocks))],
                axis=1,
            )
            total = jnp.dot(row, q, preferred_element_type=jnp.float32)
            result[at, :] = (base[at, :] + total) * factor
            copy.start()

    for copy in copies:
        copy.wait()


VMEM = functools.partial(pl.BlockSpec, memory_space=pltpu.VMEM)
SMEM = functools.partial(pl.BlockSpec, memory_space=pltpu.SMEM)


def on_device(devices, tile_blocks, q_block, tile_index, tile_count):
    tile = tile_blocks.shape[1]
    rows, columns = q_block.shape
    chips = devices // 2
    slots = chips // 2
    chip_rows = 2 * rows
    chip_blocks = chip_rows // tile
    wide = jnp.float32
    other_core = [(d, d ^ 1) for d in range(devices)]

    def swap(x):
        return lax.ppermute(x, "row", other_core)

    index = tile_index.T
    other_tiles = swap(tile_blocks)
    other_q = swap(q_block)
    other_index = swap(index)
    other_count = swap(tile_count)

    panels_shape = jax.ShapeDtypeStruct(
        ((slots + 1) * chip_blocks + 1, rows, tile), jnp.bfloat16
    )
    rows_panels_shape = jax.ShapeDtypeStruct(
        (chips * chip_blocks, rows, tile), jnp.bfloat16
    )
    q_shape = jax.ShapeDtypeStruct((chip_rows, columns), jnp.bfloat16)
    message = jax.ShapeDtypeStruct((chip_rows + 16, columns), jnp.int16)
    half_shape = jax.ShapeDtypeStruct((rows, columns), wide)
    params = pltpu.CompilerParams(vmem_limit_bytes=48 * 2**20)
    hbm = pl.BlockSpec(memory_space=pltpu.HBM)
    own = [
        pltpu.with_memory_space_constraint(a, pltpu.HBM)
        for a in (index, tile_count, tile_blocks)
    ]
    own_scratch = [
        pltpu.SMEM(index.shape, index.dtype),
        pltpu.SMEM(tile_count.shape, tile_count.dtype),
        pltpu.VMEM(tile_blocks.shape, tile_blocks.dtype),
        pltpu.SemaphoreType.DMA((3,)),
    ]
    own_panels = pl.pallas_call(
        own_kernel,
        out_shape=panels_shape,
        in_specs=[hbm] * 3,
        out_specs=VMEM(),
        scratch_shapes=own_scratch,
        compiler_params=params,
        name="own_tiles",
    )(*own)
    far = list(range(slots // 2, slots))
    near = list(reversed(range(slots // 2)))
    rest = near + far[1:]
    other = (other_index, other_count, other_tiles)
    other_specs = [pl.BlockSpec(memory_space=pl.ANY)] * 2 + [VMEM()]
    other_scratch = [*own_scratch[:2], pltpu.SemaphoreType.DMA((2,))]
    chip_q, far_message, far_panels = pl.pallas_call(
        functools.partial(far_kernel, chips, far[0]),
        out_shape=[q_shape, message, panels_shape],
        in_specs=other_specs + [VMEM()] * 3,
        out_specs=[VMEM()] * 3,
        scratch_shapes=[pltpu.VMEM((chip_blocks, tile, columns), wide), *other_scratch],
        compiler_params=params,
        name="pack_far",
    )(*other, q_block, other_q, own_panels)
    *rest_messages, mirror = pl.pallas_call(
        functools.partial(near_kernel, chips, rest),
        out_shape=[message] * len(rest) + [half_shape],
        in_specs=other_specs + [VMEM()] * 3,
        out_specs=[VMEM()] * (len(rest) + 1),
        scratch_shapes=[pltpu.VMEM(panels_shape.shape, jnp.bfloat16), *other_scratch],
        compiler_params=params,
        name="pack_near",
    )(*other, own_panels, far_panels, chip_q)
    messages = dict(zip(far[:1] + rest, [far_message, *rest_messages], strict=True))
    received = {
        k: lax.ppermute(messages[k], "row", [
            (d, d ^ (2 * cls))
            for d in range(devices)
            if (cls := class_of(k, d % 2, d < devices // 2, d // 2 % 2, chips))
        ])
        for k in far[:1] + rest
    }

    rows_panels, direct = pl.pallas_call(
        direct_kernel,
        out_shape=[rows_panels_shape, half_shape],
        in_specs=[hbm] * 3 + [VMEM()],
        out_specs=[VMEM()] * 2,
        scratch_shapes=own_scratch,
        compiler_params=params,
        cost_estimate=pl.CostEstimate(
            flops=10**10, bytes_accessed=0, transcendentals=0
        ),
        name="direct_local",
    )(*own, chip_q)

    def gather(kernel, sources, sums, name, outs, passed=()):
        sums = list(sums)
        return pl.pallas_call(
            functools.partial(kernel, chips, sources),
            out_shape=[half_shape] * outs + [message] * len(passed),
            in_specs=[VMEM()] * (1 + len(sums) + len(sources) + len(passed)),
            out_specs=[VMEM()] * (outs + len(passed)),
            input_output_aliases={
                1 + len(sums) + len(sources) + n: outs + n for n in range(len(passed))
            },
            compiler_params=params,
            cost_estimate=pl.CostEstimate(
                flops=10**10, bytes_accessed=0, transcendentals=0
            ),
            name=name,
        )(rows_panels, *sums,
          *((received if mine else other)[k] for k, mine in sources), *passed)

    *late, last = near + far[1:]
    other = {k: swap(received[k]) for k in [far[0], *late, last]}
    direct, mirror = gather(
        gather_kernel, [(far[0], True), (far[0], False)], (direct, mirror),
        "gather_first", 2,
    )
    (base,) = gather(
        join_kernel,
        [(k, mine) for k in late for mine in (True, False)] + [(last, True)],
        (direct, mirror), "gather_most", 1,
    )
    return pl.pallas_call(
        functools.partial(final_kernel, chips, last, 1.0 / math.sqrt(rows * devices)),
        out_shape=half_shape,
        in_specs=[VMEM()] * 3,
        out_specs=hbm,
        scratch_shapes=[
            pltpu.VMEM((rows, columns), wide),
            pltpu.SemaphoreType.DMA((rows // tile,)),
        ],
        compiler_params=params,
        name="gather_last",
    )(rows_panels, base, other[last])


def solution(mesh):
    return jax.shard_map(
        functools.partial(on_device, mesh.shape["row"]),
        mesh=mesh,
        in_specs=(
            P(("grp", "row"), None, None),
            P(("grp", "row"), None),
            P(("grp", "row"), None),
            P(("grp", "row")),
        ),
        out_specs=P(("grp", "row"), None),
        check_vma=False,
    )
```
